32 devices in a mesh: expert: 8 (over z, y), dp: 4 (over x, core).
Axes of the slice: x: 2, y: 2, z: 4, core: 2. Of those that a mesh axis runs over, the one named last changes fastest.
Arguments:
- grad_rows: bfloat16 [4, 4096, 2048], P('dp', 'expert'), may hold values from -6 to 6
- counts: int32 [4, 8, 8], P('dp', 'expert'), may hold values from 0 to 80, as said below
- order: int32 [4, 4096], P('dp', 'expert'), may hold values from 0 to 511, as said below
- hidden: bfloat16 [4, 8, 640, 768], P('dp', 'expert'), may hold values from -0.29882812 to 0.29882812
- down_weight: bfloat16 [8, 768, 2048], P('expert'), may hold values from -0.21875 to 0.21875
- error_in: bfloat16 [4, 8, 768, 2048], P('dp', 'expert'), may hold values from -6 to 6
- q_init: bfloat16 [8, 2048, 64], P('expert'), may hold values from -6 to 6
Outputs:
- input_grad: bfloat16 [4, 4096, 768], P('dp', 'expert')
- p_basis: float32 [8, 768, 64], P('expert')
- q_factor: float32 [8, 2048, 64], P('expert')
- error_out: bfloat16 [4, 8, 768, 2048], P('dp', 'expert')
The draws below stay inside these ranges and needn't reach their ends.
Inputs may be any that keep to these rules, and one draw needn't show every extreme that they name: On each device (r, s) the 8 counts sum to 512; in every draw one expert receives exactly 80 rows from every device. `order`: each device's 512 entries are a permutation of 0 to 511.
All inputs are finite; a program needn't handle non-finite values.
Results may differ from the reference program's by a relative error of at most 0.001.
Values may be sent and summed in bfloat16 or wider, within the bound.
No kernel may reach another device: no remote copies, remote signals or barrier semaphores. Data moves between devices by JAX's collectives and lax.ppermute only.
A program may use at most 128 MiB of HBM per device.

```python
import jax
import jax.numpy as jnp
from jax import lax

D = 2048
FF = 768
RANK = 64
ROWS_DEV = 512
EXPERTS = 8
CAP = 80
N_EXPERT = 8
N_DP = 4


def draw_counts(key, part):
    mean_rows = ROWS_DEV // EXPERTS
    spread_rows = ROWS_DEV // (4 * EXPERTS)
    devices_all = N_DP * N_EXPERT
    key_one, key_two, key_three = jax.random.split(key, 3)
    chosen = jax.random.randint(key_one, (), 0, EXPERTS)
    device_keys = jax.random.split(key_two, devices_all)
    perms = jax.vmap(lambda one_key: jax.random.permutation(one_key, EXPERTS))(device_keys).astype(jnp.int32)
    where_chosen = jnp.argmax((perms == chosen).astype(jnp.int32), axis=1)
    device_ids = jnp.arange(devices_all)
    first_ids = perms[:, 0]
    perms = perms.at[device_ids, where_chosen].set(first_ids)
    perms = perms.at[:, 0].set(chosen)
    shifts = jax.random.randint(key_three, (devices_all, EXPERTS // 2), -spread_rows, spread_rows + 1)
    shifts = shifts.at[:, 0].set(spread_rows)
    result = jnp.zeros((devices_all, EXPERTS), jnp.int32)
    result = result.at[device_ids[:, None], perms[:, 0::2]].set(mean_rows + shifts)
    result = result.at[device_ids[:, None], perms[:, 1::2]].set(mean_rows - shifts)
    return result.reshape(N_DP, N_EXPERT, EXPERTS).astype(jnp.int32)


def draw_order(key, part):
    device_keys = jax.random.split(key, N_DP * N_EXPERT)
    perms = jax.vmap(lambda one_key: jax.random.permutation(one_key, ROWS_DEV))(device_keys)
    return perms.reshape(N_DP, N_EXPERT * ROWS_DEV).astype(jnp.int32)


def block_scale(key, extent, shards, smallest, top_value):
    factor_of, own = 1.0, jax.random.fold_in(key, 6)
    for axis_at, parts in shards:
        draws = jnp.exp(jax.random.uniform(jax.random.fold_in(own, axis_at), (parts,), jnp.float32, smallest / len(shards), top_value / len(shards)))
        factor_of = factor_of * jnp.repeat(draws, extent[axis_at] // parts).reshape([-1 if axis == axis_at else 1 for axis in range(len(extent))])
    return factor_of


def scatter_about(key, extent, deviation, bound, cuts=(), held_as=jnp.bfloat16):
    drawn = deviation * jax.random.normal(key, extent, jnp.float32)
    if cuts:
        drawn = drawn * block_scale(key, extent, cuts, -0.22, 0.18)
    return jnp.clip(drawn, -bound, bound).astype(held_as)


def setup_inputs(seed: int = 0) -> dict:
    streams_of = jax.random.split(jax.random.key(seed), 8)
    grad_rows = scatter_about(streams_of[0], (N_DP, N_EXPERT * ROWS_DEV, D), 1.0, 6.0, ((0, 4), (1, 8)))
    counts = draw_counts(jax.random.fold_in(streams_of[7], 71), 0)
    order = draw_order(jax.random.fold_in(streams_of[7], 71), 0)
    hidden = scatter_about(streams_of[3], (N_DP, EXPERTS, N_EXPERT * CAP, FF), 0.05, 0.29882812, ((0, 4), (1, 8)))
    down_weight = scatter_about(streams_of[4], (EXPERTS, FF, D), FF ** -0.5, 0.21875, ((0, 8),))
    error_in = scatter_about(streams_of[5], (N_DP, EXPERTS, FF, D), 1.0, 6.0, ((0, 4), (1, 8)))
    q_init = scatter_about(streams_of[6], (EXPERTS, D, RANK), 1.0, 6.0, ((0, 8),))
    return {"grad_rows": grad_rows, "counts": counts, "order": order, "hidden": hidden, "down_weight": down_weight, "error_in": error_in, "q_init": q_init}


def orthonormal(p_total):
    gram = jnp.dot(p_total.T, p_total, precision=lax.Precision.HIGHEST)
    lower = jnp.linalg.cholesky(gram)
    return lax.linalg.triangular_solve(lower, p_total, left_side=False, lower=True, transpose_a=True)

def reference(grad_rows, counts, order, hidden, down_weight, error_in, q_init):
    recv_rows = N_EXPERT * CAP
    route_ends = jnp.cumsum(counts, axis=2).astype(jnp.int32)
    route_starts = (route_ends - counts).astype(jnp.int32)
    slot_ids = jnp.arange(CAP, dtype=jnp.int32)
    source_ids = jnp.arange(N_EXPERT, dtype=jnp.int32)

    def one_expert(expert_id):
        start_now = route_starts[:, :, expert_id]
        count_now = counts[:, :, expert_id]
        pick_index = source_ids[None, :, None] * ROWS_DEV + start_now[:, :, None] + slot_ids[None, None, :]
        pick_index = jnp.minimum(pick_index, N_EXPERT * ROWS_DEV - 1).astype(jnp.int32)
        slot_valid = slot_ids[None, None, :] < count_now[:, :, None]
        picked = jax.vmap(lambda table, where_rows: table[where_rows])(grad_rows, pick_index.reshape(N_DP, recv_rows))
        picked = jnp.where(slot_valid.reshape(N_DP, recv_rows, 1), picked, jnp.zeros((), jnp.bfloat16))
        expert_weight = down_weight[expert_id]
        q_start = q_init[expert_id].astype(jnp.float32)
        back_list = []
        moment_list = []
        for replica in range(N_DP):
            saved_hidden = hidden[replica, expert_id]
            grad_w = jnp.dot(saved_hidden.T.astype(jnp.float32), picked[replica].astype(jnp.float32), preferred_element_type=jnp.float32)
            back_list.append(jnp.dot(picked[replica].astype(jnp.float32), expert_weight.T.astype(jnp.float32), preferred_element_type=jnp.float32).astype(jnp.bfloat16))
            moment_list.append(grad_w + error_in[replica, expert_id].astype(jnp.float32))
        p_total = jnp.dot(moment_list[0], q_start, precision=lax.Precision.HIGHEST)
        for replica in range(1, N_DP):
            p_total = p_total + jnp.dot(moment_list[replica], q_start, precision=lax.Precision.HIGHEST)
        p_basis = orthonormal(p_total)
        q_total = jnp.dot(moment_list[0].T, p_basis, precision=lax.Precision.HIGHEST)
        for replica in range(1, N_DP):
            q_total = q_total + jnp.dot(moment_list[replica].T, p_basis, precision=lax.Precision.HIGHEST)
        q_factor = q_total / N_DP
        approximation = jnp.dot(p_basis, q_factor.T, precision=lax.Precision.HIGHEST)
        errors = jnp.stack([(moment - approximation).astype(jnp.bfloat16) for moment in moment_list])
        return (jnp.stack(back_list), p_basis, q_factor, errors)
    backs, bases, q_factors, errors = lax.map(one_expert, jnp.arange(EXPERTS, dtype=jnp.int32))
    flat_back = backs.reshape(EXPERTS * N_DP * recv_rows, FF)
    source_pos = order.reshape(N_DP, N_EXPERT, ROWS_DEV)
    expert_of = jnp.sum((route_ends[:, :, None, :] <= source_pos[:, :, :, None]).astype(jnp.int32), axis=3).astype(jnp.int32)
    start_of = jnp.take_along_axis(route_starts, expert_of, axis=2)
    replica_ids = jnp.arange(N_DP, dtype=jnp.int32)[:, None, None]
    owner_ids = jnp.arange(N_EXPERT, dtype=jnp.int32)[None, :, None]
    position = (expert_of * N_DP + replica_ids) * recv_rows + owner_ids * CAP + source_pos - start_of
    input_grad = flat_back[position.reshape(-1).astype(jnp.int32)].reshape(N_DP, N_EXPERT * ROWS_DEV, FF)
    return (input_grad, bases, q_factors, jnp.transpose(errors, (1, 0, 2, 3)))
```

```python
import functools

import jax
import jax.numpy as jnp
from jax import lax
from jax.experimental import pallas as pl
from jax.experimental.pallas import tpu as pltpu
from jax.sharding import PartitionSpec as P

F32 = jnp.float32
BF16 = jnp.bfloat16
ROW_TILE = 16
COLS = 512
MIB = 1024 * 1024
FULL = 58


def whole_vmem():
    return pl.BlockSpec(memory_space=pltpu.VMEM)


def split3(x):
    hi = x.astype(BF16)
    rest = x - hi.astype(F32)
    mid = rest.astype(BF16)
    lo = (rest - mid.astype(F32)).astype(BF16)
    return hi, mid, lo


def stack3(x):
    return jnp.concatenate(split3(x), axis=0)


def fold3(x):
    n = x.shape[0] // 3
    return x[:n] + (x[n : 2 * n] + x[2 * n :])


def dot_nt(a, b):
    return lax.dot_general(a, b, (((1,), (1,)), ((), ())), preferred_element_type=F32)


def dot_nn(a, b):
    return jnp.dot(a, b, preferred_element_type=F32)


def full_dot(a, b):
    return jnp.dot(a, b, precision=lax.Precision.HIGHEST, preferred_element_type=F32)

def in_hbm():
    return pl.BlockSpec(memory_space=pltpu.HBM)


TOKEN = ((8, 128), F32)


def set_token(ref):
    ref[...] = jnp.zeros(ref.shape, ref.dtype)


def cost(flops, nbytes):
    return pl.CostEstimate(flops=flops, bytes_accessed=nbytes, transcendentals=0)


def call(kernel, name, scalars, operands, outs, scratch=(), limit=12, flops=10**9, nbytes=10**6, specs=None, out_specs=None):
    outs = [jax.ShapeDtypeStruct(shape, dtype) for shape, dtype in outs]
    return pl.pallas_call(
        kernel,
        grid_spec=pltpu.PrefetchScalarGridSpec(
            num_scalar_prefetch=len(scalars),
            grid=(),
            in_specs=specs or [whole_vmem()] * len(operands),
            out_specs=out_specs or [whole_vmem()] * len(outs),
            scratch_shapes=list(scratch),
        ),
        out_shape=outs,
        compiler_params=pltpu.CompilerParams(vmem_limit_bytes=limit * MIB),
        cost_estimate=cost(flops, nbytes),
        name=name,
    )(*scalars, *operands)


def pack_kernel(n, cap, masks, me_ref, core_ref, counts_hbm, rows_hbm, *rest):
    outs = rest[: len(masks)]
    counts_ref, rows_ref, held, sems, out_sems = rest[len(masks) :]
    total = rows_ref.shape[0]
    window = -(-(cap + ROW_TILE - 1) // ROW_TILE) * ROW_TILE
    copy_counts = pltpu.make_async_copy(counts_hbm, counts_ref, sems.at[0])
    copy_rows = pltpu.make_async_copy(rows_hbm, rows_ref, sems.at[1])
    copy_counts.start()
    copy_rows.start()
    copy_counts.wait()
    j = lax.broadcasted_iota(jnp.int32, (cap, window), 0)
    w = lax.broadcasted_iota(jnp.int32, (cap, window), 1)
    bases, picks = [], []
    for mask in masks:
        dest = me_ref[0] ^ mask
        start = jnp.int32(0)
        for e in range(n):
            start = start + jnp.where(e < dest, counts_ref[0, e], 0)
        base = jnp.minimum((start // ROW_TILE) * ROW_TILE, total - window)
        bases.append(pl.multiple_of(base, ROW_TILE))
        hit = (w == j + (start - base)) & (j < counts_ref[0, dest])
        picks.append(jnp.where(hit, 1.0, 0.0).astype(BF16))
    copy_rows.wait()
    if len(masks) == 1:
        outs[0][...] = dot_nn(picks[0], rows_ref[pl.ds(bases[0], window), :]).astype(BF16)
        return
    copies = []
    for k, (base, pick) in enumerate(zip(bases, picks)):
        held[k] = dot_nn(pick, rows_ref[pl.ds(base, window), :]).astype(BF16)
        copies.append(pltpu.make_async_copy(held.at[k], outs[k], out_sems.at[k]))
        copies[k].start()
    for copy in copies:
        copy.wait()


def pack(me, core, counts, rows, n, cap, masks, nbytes, out_spec, limit):
    count, width = len(masks), rows.shape[1]
    return call(
        functools.partial(pack_kernel, n, cap, masks),
        "pack_rows",
        (me, core),
        (counts, rows),
        [((cap, width), BF16)] * count,
        [
            pltpu.SMEM(counts.shape, jnp.int32),
            pltpu.VMEM(rows.shape, BF16),
            pltpu.VMEM((count, cap, width), BF16),
            pltpu.SemaphoreType.DMA((2,)),
            pltpu.SemaphoreType.DMA((count,)),
        ],
        specs=[in_hbm()] * 2,
        out_specs=[out_spec] * count,
        limit=limit,
        flops=10**6,
        nbytes=nbytes,
    )


def source_at(me_ref, slot, cap):
    if slot is None:
        return 0
    return pl.multiple_of((me_ref[0] ^ slot) * cap, ROW_TILE)


def place(chunks, slots, me_ref, hidden_ref, both_ref, at):
    cap, width = chunks[0].shape
    for k, slot in enumerate(slots):
        rows = pl.ds(at + k * cap, cap)
        both_ref[rows, :width] = chunks[k][...]
        both_ref[rows, width:] = hidden_ref[pl.ds(source_at(me_ref, slot, cap), cap), :]


def p_term(q, rows, hidden):
    return fold3(dot_nn(stack3(dot_nt(q, rows)), hidden))


def early_kernel(slots, me_ref, q_ref, hidden_ref, error_ref, weight_ref, *rest):
    chunks = rest[: len(slots)]
    p_ref, both_ref, moment_ref, *slot_refs = rest[len(slots) :]
    cap = chunks[0].shape[0]
    width = error_ref.shape[1]
    place(chunks, slots, me_ref, hidden_ref, both_ref, 0)
    q = q_ref[...]
    p_ref[...] = dot_nt(q, error_ref[...]) + p_term(q, both_ref[:, :width], both_ref[:, width:])
    hidden_t = both_ref[:, width:].T
    for j in range(0, width, COLS):
        block = dot_nn(hidden_t, both_ref[:, j : j + COLS])
        moment_ref[:, j : j + COLS] = error_ref[:, j : j + COLS].astype(F32) + block
    res = dot_nt(both_ref[:, :width], weight_ref[...]).astype(BF16)
    for k, ref in enumerate(slot_refs):
        ref[...] = res[k * cap : (k + 1) * cap]


def early_part(me, q, hidden, error, weight, chunks, slots):
    cap, width = chunks[0].shape
    ff = hidden.shape[1]
    rows = cap * len(slots)
    return call(
        functools.partial(early_kernel, slots),
        "early_rows",
        (me,),
        (q, hidden, error, weight, *chunks),
        [((q.shape[0], ff), F32), ((rows, width + ff), BF16), ((ff, width), F32)]
        + [((cap, ff), BF16)] * len(slots),
        flops=2 * 10**9,
        nbytes=10**7,
    )


def late_kernel(slots, me_ref, q_ref, hidden_ref, base_ref, *rest):
    chunks, (p_ref, both_ref) = rest[: len(slots)], rest[len(slots) :]
    width = chunks[0].shape[1]
    place(chunks, slots, me_ref, hidden_ref, both_ref, 0)
    p_ref[...] = base_ref[...] + p_term(q_ref[...], both_ref[:, :width], both_ref[:, width:])


def late_part(me, q, hidden, base, chunks, slots):
    cap, width = chunks[0].shape
    ff = hidden.shape[1]
    return call(
        functools.partial(late_kernel, slots),
        "late_rows",
        (me,),
        (q, hidden, base, *chunks),
        [((q.shape[0], ff), F32), ((cap * len(slots), width + ff), BF16)],
        flops=10**6,
        nbytes=10**4,
    )


def slot_kernel(at, count, both_ref, weight_ref, *rest):
    outs = rest[len(rest) - count :]
    cap, width = outs[0].shape[0], weight_ref.shape[1]
    res = dot_nt(both_ref[at : at + cap * count, :width], weight_ref[...]).astype(BF16)
    for k, out in enumerate(outs):
        out[...] = res[k * cap : (k + 1) * cap]


def slot_grads(both, weight, before, at, cap, count, flops):
    return call(
        functools.partial(slot_kernel, at, count),
        "slot_grads",
        (),
        (both, weight, *before),
        [((cap, weight.shape[0]), BF16)] * count,
        flops=flops,
        nbytes=10**4,
    )


def s_kernel(core_ref, pa_ref, pb_ref, error_ref, *rest):
    *groups, p_out, send_ref, keep_ref, token_ref = rest
    set_token(token_ref)
    total = pa_ref[...] + pb_ref[...]
    p_out[...] = total
    p3 = stack3(total)
    width = error_ref.shape[1]
    half = width // 2
    ys = [stack3(fold3(dot_nt(p3, group[:, width:]))) for group in groups]
    for out, part in ((send_ref, 1 - core_ref[0]), (keep_ref, core_ref[0])):
        for j in range(0, half, COLS):
            cols = pl.ds(pl.multiple_of(part * half + j, COLS), COLS)
            res = dot_nn(p3, error_ref[:, cols])
            for y, group in zip(ys, groups):
                res = res + dot_nn(y, group[:, cols])
            out[:, j : j + COLS] = fold3(res)


def s_partial(core, pa, pb, error, groups):
    rank, ff = pa.shape
    width = error.shape[1]
    return call(
        s_kernel,
        "s_partial",
        (core,),
        (pa, pb, error, *groups),
        [((rank, ff), F32), ((rank, width // 2), F32), ((rank, width // 2), F32), TOKEN],
        nbytes=7 * 10**6,
    )


def basis_kernel(p_ref, before_ref, basis_ref, linv_ref, left_ref):
    p = p_ref[...]
    rank = p.shape[0]
    p3 = stack3(p)
    gram_rows = fold3(dot_nt(p3, p3))
    gram = gram_rows[:, :rank] + (gram_rows[:, rank : 2 * rank] + gram_rows[:, 2 * rank :])
    row = lax.broadcasted_iota(jnp.int32, (rank, rank), 0)
    col = lax.broadcasted_iota(jnp.int32, (rank, rank), 1)
    eye = jnp.where(row == col, 1.0, 0.0)
    aug = jnp.concatenate([gram, eye], axis=1)
    sub, group = 8, 4
    shape = (sub, 2 * rank)
    blocks = [aug[b * sub : (b + 1) * sub] for b in range(rank // sub)]
    sub_id = lax.broadcasted_iota(jnp.int32, shape, 0)
    for k in range(0, rank, group):
        kb, kr = divmod(k, sub)
        spread = {
            (b, i): jnp.broadcast_to(blocks[b][:, k + i : k + i + 1], shape)
            for b in range(kb, rank // sub)
            for i in range(group)
        }
        low, scale, pivots = {}, [], []
        for i in range(group):
            for j in range(i + 1):
                left = jnp.broadcast_to(spread[kb, j][kr + i : kr + i + 1], shape)
                for m in range(j):
                    left = left - low[i, m] * low[j, m]
                low[i, j] = left * scale[j] if j < i else left
            scale.append(lax.rsqrt(low[i, i]))
            pivot = jnp.broadcast_to(blocks[kb][kr + i : kr + i + 1], shape)
            for m in range(i):
                pivot = pivot - low[i, m] * pivots[m]
            pivots.append(pivot * scale[i])
        for b in range(kb, rank // sub):
            updated, factors = blocks[b], []
            for i in range(group):
                factor = spread[b, i]
                for m in range(i):
                    factor = factor - factors[m] * low[i, m]
                factors.append(factor * scale[i])
                updated = updated - factors[i] * pivots[i]
            if b == kb:
                updated = jnp.where(sub_id >= kr + group, updated, blocks[b])
                for i in range(group):
                    updated = jnp.where(sub_id == kr + i, pivots[i], updated)
            blocks[b] = updated
    linv = jnp.concatenate(blocks, axis=0)[:, rank:]
    linv_ref[...] = linv
    basis = full_dot(linv, p)
    basis_ref[...] = basis
    hi, mid, lo = split3(basis)
    left_ref[...] = jnp.concatenate([hi, hi, mid, mid, hi, lo], axis=0).T


def basis_of(p, before):
    rank, ff = p.shape
    return call(
        basis_kernel,
        "basis",
        (),
        (p, before),
        [((rank, ff), F32), ((rank, rank), F32), ((ff, 6 * rank), BF16)],
        flops=10**10,
    )


def moment_kernel(before_ref, moment_ref, both_ref, out_ref):
    width = out_ref.shape[1]
    hidden_t = both_ref[:, width:].T
    for j in range(0, width, COLS):
        cols = slice(j, j + COLS)
        out_ref[:, cols] = moment_ref[:, cols] + dot_nn(hidden_t, both_ref[:, cols])


def moment_add(before, moment, both):
    return call(
        moment_kernel,
        "moment_add",
        (),
        (before, moment, both),
        [(moment.shape, F32)],
        nbytes=10**7,
    )[0]


def q_kernel(replicas, mine_ref, far_ref, linv_ref, out_ref):
    out_ref[...] = full_dot(linv_ref[...], mine_ref[...] + far_ref[...]) * (1.0 / replicas)


def q_half(mine, far, linv, replicas):
    return call(functools.partial(q_kernel, replicas), "q_half", (), (mine, far, linv), [(mine.shape, F32)])[0]


def error_block(part, k, block, q_ref, left_ref, moment_ref, right):
    rank, half = q_ref.shape
    here = pl.ds(k * block, block)
    cols = pl.ds(pl.multiple_of(part * half + k * block, block), block)
    hi, mid, lo = split3(-q_ref[:, here])
    for i, piece in enumerate((hi, mid, hi, mid, lo, hi)):
        right[i * rank : (i + 1) * rank, here] = piece
    return (moment_ref[:, cols] + dot_nn(left_ref[...], right[:, here])).astype(BF16)


def error_first_kernel(block, core_ref, q_ref, left_ref, moment_ref, out_ref, right):
    for k in range(q_ref.shape[1] // block):
        here = pl.ds(k * block, block)
        out_ref[:, here] = error_block(core_ref[0], k, block, q_ref, left_ref, moment_ref, right)


def error_first(core, q, left, moment):
    half = q.shape[1]
    return call(
        functools.partial(error_first_kernel, 256),
        "new_error_first",
        (core,),
        (q, left, moment),
        [((moment.shape[0], half), BF16)],
        [pltpu.VMEM((left.shape[1], half), BF16)],
        flops=10**10,
    )[0]


def error_second_kernel(block, core_ref, mine_ref, other_ref, left_ref, moment_ref, first_ref, *rest):
    q_hbm, out_hbm, token_ref, right, held, sems = rest
    set_token(token_ref)
    half = mine_ref.shape[1]
    part = 1 - core_ref[0]
    at_mine = pl.ds(pl.multiple_of(core_ref[0] * half, half), half)
    at_other = pl.ds(pl.multiple_of(part * half, half), half)
    copies = [
        pltpu.make_async_copy(first_ref, out_hbm.at[:, at_mine], sems.at[0]),
        pltpu.make_async_copy(mine_ref, q_hbm.at[:, at_mine], sems.at[1]),
        pltpu.make_async_copy(other_ref, q_hbm.at[:, at_other], sems.at[2]),
    ]
    for copy in copies:
        copy.start()
    for k in range(half // block):
        here = pl.ds(k * block, block)
        cols = pl.ds(pl.multiple_of(part * half + k * block, block), block)
        held[:, here] = error_block(part, k, block, other_ref, left_ref, moment_ref, right)
        copies.append(pltpu.make_async_copy(held.at[:, here], out_hbm.at[:, cols], sems.at[3 + k]))
        copies[-1].start()
    for copy in copies:
        copy.wait()


def error_second(core, mine, other, left, moment, first):
    ff, width = moment.shape
    rank, half = mine.shape
    block = 256
    return call(
        functools.partial(error_second_kernel, block),
        "new_error_second",
        (core,),
        (mine, other, left, moment, first),
        [((rank, width), F32), ((ff, width), BF16), TOKEN],
        [
            pltpu.VMEM((left.shape[1], half), BF16),
            pltpu.VMEM((ff, half), BF16),
            pltpu.SemaphoreType.DMA((3 + half // block,)),
        ],
        out_specs=[in_hbm(), in_hbm(), whole_vmem()],
        flops=10**10,
    )


def pick_kernel(n, cap, masks, me_ref, counts_ref, order_ref, out_ref, held):
    order = order_ref[...]
    j = lax.broadcasted_iota(jnp.int32, (cap, order.shape[1]), 0)
    for k, mask in enumerate(masks):
        expert = me_ref[0] ^ mask
        start = jnp.int32(0)
        for e in range(n):
            start = start + jnp.where(e < expert, counts_ref[e], 0)
        hit = (order == j + start) & (j < counts_ref[expert])
        held[k * cap : (k + 1) * cap, :] = jnp.where(hit, 1.0, 0.0)
    out_ref[...] = held[...].T.astype(BF16)


def pick_of(me, counts, order, n, cap, masks):
    tokens = order.shape[1]
    slots = len(masks) * cap
    return call(
        functools.partial(pick_kernel, n, cap, masks),
        "pick_rows",
        (me, counts),
        (order,),
        [((tokens, slots), BF16)],
        [pltpu.VMEM((slots, tokens), F32)],
        flops=10**6,
        nbytes=10**4,
    )[0]


def unpack_first_kernel(count, before_ref, pick_ref, *rest):
    chunks, (out_ref, token_ref, cat) = rest[:count], rest[count:]
    cap = chunks[0].shape[0]
    for k in range(count):
        cat[k * cap : (k + 1) * cap, :] = chunks[k][...]
    out_ref[...] = dot_nn(pick_ref[...], cat[...]).astype(BF16)
    set_token(token_ref)


def unpack_first(before, pick, chunks):
    cap, ff = chunks[0].shape
    return call(
        functools.partial(unpack_first_kernel, len(chunks)),
        "unpack_first",
        (),
        (before, pick, *chunks),
        [((pick.shape[0], ff), BF16), TOKEN],
        [pltpu.VMEM((len(chunks) * cap, ff), BF16)],
        flops=10**10,
    )


def unpack_kernel(count, parts, token_ref, pick_ref, first_ref, *rest):
    chunks, (out_hbm, cat, out_ref, sems) = rest[:count], rest[count:]
    cap = chunks[0].shape[0]
    for k in range(count):
        cat[k * cap : (k + 1) * cap, :] = chunks[k][...]
    rows = out_ref.shape[0] // parts
    copies = []
    for k in range(parts):
        at = pl.ds(k * rows, rows)
        out_ref[at, :] = first_ref[at, :] + dot_nn(pick_ref[at, :], cat[...]).astype(BF16)
        copies.append(pltpu.make_async_copy(out_ref.at[at, :], out_hbm.at[at, :], sems.at[k]))
        copies[k].start()
    for copy in copies:
        copy.wait()


def unpack(token, pick, first, chunks):
    cap, ff = chunks[0].shape
    tokens, slots = pick.shape
    parts = 2
    return pl.pallas_call(
        functools.partial(unpack_kernel, len(chunks), parts),
        in_specs=[whole_vmem()] * (3 + len(chunks)),
        out_specs=in_hbm(),
        out_shape=jax.ShapeDtypeStruct((tokens, ff), BF16),
        scratch_shapes=[
            pltpu.VMEM((slots, ff), BF16),
            pltpu.VMEM((tokens, ff), BF16),
            pltpu.SemaphoreType.DMA((parts,)),
        ],
        compiler_params=pltpu.CompilerParams(vmem_limit_bytes=8 * MIB),
        cost_estimate=cost(10**6, 10**4),
        name="unpack_rows",
    )(token, pick, first, *chunks)


def pack_plain(route_count, local_rows, experts, capacity):
    total_rows, width = local_rows.shape
    route_starts = jnp.cumsum(route_count) - route_count
    slot_ids = jnp.arange(capacity, dtype=jnp.int32)
    pick_index = jnp.minimum(route_starts[:, None] + slot_ids[None, :], total_rows - 1)
    slot_valid = slot_ids[None, :] < route_count[:, None]
    outgoing = local_rows[pick_index.reshape(-1)].reshape(experts, capacity, width)
    return jnp.where(slot_valid[:, :, None], outgoing, jnp.zeros((), BF16))


def unpack_plain(route_count, order_local, returned, experts, capacity):
    route_ends = jnp.cumsum(route_count)
    route_starts = route_ends - route_count
    expert_of = jnp.sum((route_ends[None, :] <= order_local[:, None]).astype(jnp.int32), axis=1)
    row_base = jnp.arange(experts, dtype=jnp.int32) * capacity - route_starts
    return returned[row_base[expert_of] + order_local]


def add_kernel(a_ref, b_ref, *rest):
    rest[-1][...] = a_ref[...] + b_ref[...]


def add(a, b, *before):
    return call(add_kernel, "add", (), (a, b, *before), [(a.shape, F32)], limit=4, flops=10**6)[0]


def pass_kernel(x_ref, before_ref, out_ref):
    out_ref[...] = x_ref[...]


def pass_on(x, before):
    return call(pass_kernel, "pass_on", (), (x, before), [(x.shape, x.dtype)], limit=4, flops=10**6)[0]


def shards(n_expert, n_dp, grad_rows, counts, order, hidden, down_weight, error_in, q_init):
    rows = grad_rows[0]
    count = counts[0, 0]
    saved = hidden[0, 0]
    weight = down_weight[0]
    error = error_in[0, 0]
    q = q_init[0].T
    ff = saved.shape[1]
    capacity = saved.shape[0] // n_expert
    me = lax.axis_index("expert").astype(jnp.int32)[None]
    core = (lax.axis_index("dp").astype(jnp.int32) & 1)[None]
    core_pairs = [(d, d ^ 1) for d in range(n_dp)]
    chip_pairs = [(d, d ^ 2) for d in range(n_dp)]
    by_pairs = n_expert == 8 and capacity % ROW_TILE == 0

    if by_pairs:
        far = tuple(reversed(range(n_expert // 2, n_expert)))
        near = tuple(reversed(range(0, n_expert // 2)))
        first, last = far[:1] + near, far[1:]

        def swap(x, mask):
            return lax.ppermute(x, "expert", [(e, e ^ mask) for e in range(n_expert)])

        others = far[1:] + near
        packed = {far[0]: pack(me, core, counts[0], rows, n_expert, capacity, far[:1], 4 * 10**6, whole_vmem(), 62)[0]}
        packed.update(zip(others, pack(me, core, counts[0], rows, n_expert, capacity, others, 10**4, in_hbm(), FULL)))
        arrived = {m: swap(packed[m], m) if m else packed[m] for m in far + near}
        pick_near = pick_of(me, count, order, n_expert, capacity, near)
        pick_far = pick_of(me, count, order, n_expert, capacity, far)
        p_first, both_first, moment, *back = early_part(
            me, q, saved, error, weight, [arrived[m] for m in first], first
        )
        back_near = [swap(x, m) if m else x for x, m in zip(back[1:], near)]
        p_mine, both_last = late_part(me, q, saved, p_first, [arrived[m] for m in last], last)
        back_next = slot_grads(
            both_last, weight, (pick_near, pick_far, *back_near), 0, capacity, len(last), 10**10
        )
        before, groups = back_next[:1], [both_first, both_last]
    else:
        outgoing = pack_plain(count, rows, n_expert, capacity)
        arrived = lax.all_to_all(outgoing, "expert", split_axis=0, concat_axis=0, tiled=True)
        arrived = arrived.reshape(n_expert * capacity, rows.shape[1])
        p_mine, both_first, moment, back = early_part(me, q, saved, error, weight, [arrived], (None,))
        before, groups = [], [both_first]
        back = back.reshape(n_expert, capacity, ff)
        returned = lax.all_to_all(back, "expert", split_axis=0, concat_axis=0, tiled=True)
        returned = returned.reshape(n_expert * capacity, ff)
    p_chip = add(p_mine, lax.ppermute(p_mine, "dp", core_pairs), *before)
    p_far = lax.ppermute(p_chip, "dp", chip_pairs)
    p_total, s_send, s_keep, token = s_partial(core, p_chip, p_far, error, groups)
    if by_pairs:
        grad_near, token = unpack_first(token, pick_near, back_near)
    s_half = add(s_keep, lax.ppermute(s_send, "dp", core_pairs), token)
    if by_pairs:
        back_last = pass_on(back_next[-1], s_half)
        back_far = [swap(x, m) for x, m in zip([back[0], *back_next[:-1], back_last], far)]
        moment = moment_add(back_last, moment, both_last)
    basis, linv, left = basis_of(p_total, moment)
    q_mine = q_half(s_half, lax.ppermute(s_half, "dp", chip_pairs), linv, n_dp)
    q_other = lax.ppermute(q_mine, "dp", core_pairs)
    first_half = error_first(core, q_mine, left, moment)
    q_factor, error_out, token = error_second(core, q_mine, q_other, left, moment, first_half)
    if by_pairs:
        input_grad = unpack(token, pick_far, grad_near, back_far)
    else:
        input_grad = unpack_plain(count, order[0], returned, n_expert, capacity)
    return (input_grad[None], basis.T[None], q_factor.T[None], error_out[None, None])


def solution(mesh):
    placed = (
        P("dp", "expert", None),
        P("dp", "expert", None),
        P("dp", "expert"),
        P("dp", "expert", None, None),
        P("expert", None, None),
        P("dp", "expert", None, None),
        P("expert", None, None),
    )
    return jax.shard_map(
        functools.partial(shards, mesh.shape["expert"], mesh.shape["dp"]),
        mesh=mesh,
        in_specs=placed,
        out_specs=(
            P("dp", "expert", None),
            P("expert", None, None),
            P("expert", None, None),
            P("dp", "expert", None, None),
        ),
        check_vma=False,
    )
```

```python
import functools

import jax
import jax.numpy as jnp
from jax import lax
from jax.experimental import pallas as pl
from jax.experimental.pallas import tpu as pltpu
from jax.sharding import PartitionSpec as P

F32 = jnp.float32
BF16 = jnp.bfloat16
ROW_TILE = 16
COLS = 512
MIB = 1024 * 1024
FULL = 58


def whole_vmem():
    return pl.BlockSpec(memory_space=pltpu.VMEM)


def split3(x):
    hi = x.astype(BF16)
    rest = x - hi.astype(F32)
    mid = rest.astype(BF16)
    lo = (rest - mid.astype(F32)).astype(BF16)
    return hi, mid, lo


def stack3(x):
    return jnp.concatenate(split3(x), axis=0)


def fold3(x):
    n = x.shape[0] // 3
    return x[:n] + (x[n : 2 * n] + x[2 * n :])


def dot_nt(a, b):
    return lax.dot_general(a, b, (((1,), (1,)), ((), ())), preferred_element_type=F32)


def dot_nn(a, b):
    return jnp.dot(a, b, preferred_element_type=F32)


def full_dot(a, b):
    return jnp.dot(a, b, precision=lax.Precision.HIGHEST, preferred_element_type=F32)

def in_hbm():
    return pl.BlockSpec(memory_space=pltpu.HBM)


TOKEN = ((8, 128), F32)


def set_token(ref):
    ref[...] = jnp.zeros(ref.shape, ref.dtype)


def cost(flops, nbytes):
    return pl.CostEstimate(flops=flops, bytes_accessed=nbytes, transcendentals=0)


def call(kernel, name, scalars, operands, outs, scratch=(), limit=12, flops=10**9, nbytes=10**6, specs=None, out_specs=None):
    outs = [jax.ShapeDtypeStruct(shape, dtype) for shape, dtype in outs]
    return pl.pallas_call(
        kernel,
        grid_spec=pltpu.PrefetchScalarGridSpec(
            num_scalar_prefetch=len(scalars),
            grid=(),
            in_specs=specs or [whole_vmem()] * len(operands),
            out_specs=out_specs or [whole_vmem()] * len(outs),
            scratch_shapes=list(scratch),
        ),
        out_shape=outs,
        compiler_params=pltpu.CompilerParams(vmem_limit_bytes=limit * MIB),
        cost_estimate=cost(flops, nbytes),
        name=name,
    )(*scalars, *operands)


def pack_kernel(n, cap, masks, me_ref, core_ref, counts_hbm, rows_hbm, *rest):
    outs = rest[: len(masks)]
    counts_ref, rows_ref, held, sems, out_sems = rest[len(masks) :]
    total = rows_ref.shape[0]
    window = -(-(cap + ROW_TILE - 1) // ROW_TILE) * ROW_TILE
    copy_counts = pltpu.make_async_copy(counts_hbm, counts_ref, sems.at[0])
    copy_rows = pltpu.make_async_copy(rows_hbm, rows_ref, sems.at[1])
    copy_counts.start()
    copy_rows.start()
    copy_counts.wait()
    j = lax.broadcasted_iota(jnp.int32, (cap, window), 0)
    w = lax.broadcasted_iota(jnp.int32, (cap, window), 1)
    bases, picks = [], []
    for mask in masks:
        dest = me_ref[0] ^ mask
        start = jnp.int32(0)
        for e in range(n):
            start = start + jnp.where(e < dest, counts_ref[0, e], 0)
        base = jnp.minimum((start // ROW_TILE) * ROW_TILE, total - window)
        bases.append(pl.multiple_of(base, ROW_TILE))
        hit = (w == j + (start - base)) & (j < counts_ref[0, dest])
        picks.append(jnp.where(hit, 1.0, 0.0).astype(BF16))
    copy_rows.wait()
    if len(masks) == 1:
        outs[0][...] = dot_nn(picks[0], rows_ref[pl.ds(bases[0], window), :]).astype(BF16)
        return
    copies = []
    for k, (base, pick) in enumerate(zip(bases, picks)):
        held[k] = dot_nn(pick, rows_ref[pl.ds(base, window), :]).astype(BF16)
        copies.append(pltpu.make_async_copy(held.at[k], outs[k], out_sems.at[k]))
        copies[k].start()
    for copy in copies:
        copy.wait()


def pack(me, core, counts, rows, n, cap, masks, nbytes, out_spec, limit):
    count, width = len(masks), rows.shape[1]
    return call(
        functools.partial(pack_kernel, n, cap, masks),
        "pack_rows",
        (me, core),
        (counts, rows),
        [((cap, width), BF16)] * count,
        [
            pltpu.SMEM(counts.shape, jnp.int32),
            pltpu.VMEM(rows.shape, BF16),
            pltpu.VMEM((count, cap, width), BF16),
            pltpu.SemaphoreType.DMA((2,)),
            pltpu.SemaphoreType.DMA((count,)),
        ],
        specs=[in_hbm()] * 2,
        out_specs=[out_spec] * count,
        limit=limit,
        flops=10**6,
        nbytes=nbytes,
    )


def source_at(me_ref, slot, cap):
    if slot is None:
        return 0
    return pl.multiple_of((me_ref[0] ^ slot) * cap, ROW_TILE)


def place(chunks, slots, me_ref, hidden_ref, both_ref, at):
    cap, width = chunks[0].shape
    for k, slot in enumerate(slots):
        rows = pl.ds(at + k * cap, cap)
        both_ref[rows, :width] = chunks[k][...]
        both_ref[rows, width:] = hidden_ref[pl.ds(source_at(me_ref, slot, cap), cap), :]


def p_term(q, rows, hidden):
    return fold3(dot_nn(stack3(dot_nt(q, rows)), hidden))


def early_kernel(slots, me_ref, q_ref, hidden_ref, error_ref, weight_ref, *rest):
    chunks = rest[: len(slots)]
    p_ref, both_ref, moment_ref, *slot_refs = rest[len(slots) :]
    cap = chunks[0].shape[0]
    width = error_ref.shape[1]
    place(chunks, slots, me_ref, hidden_ref, both_ref, 0)
    q = q_ref[...]
    p_ref[...] = dot_nt(q, error_ref[...]) + p_term(q, both_ref[:, :width], both_ref[:, width:])
    hidden_t = both_ref[:, width:].T
    for j in range(0, width, COLS):
        block = dot_nn(hidden_t, both_ref[:, j : j + COLS])
        moment_ref[:, j : j + COLS] = error_ref[:, j : j + COLS].astype(F32) + block
    res = dot_nt(both_ref[:, :width], weight_ref[...]).astype(BF16)
    for k, ref in enumerate(slot_refs):
        ref[...] = res[k * cap : (k + 1) * cap]


def early_part(me, q, hidden, error, weight, chunks, slots):
    cap, width = chunks[0].shape
    ff = hidden.shape[1]
    rows = cap * len(slots)
    return call(
        functools.partial(early_kernel, slots),
        "early_rows",
        (me,),
        (q, hidden, error, weight, *chunks),
        [((q.shape[0], ff), F32), ((rows, width + ff), BF16), ((ff, width), F32)]
        + [((cap, ff), BF16)] * len(slots),
        flops=2 * 10**9,
        nbytes=10**7,
    )


def late_kernel(slots, me_ref, q_ref, hidden_ref, base_ref, *rest):
    chunks, (p_ref, both_ref) = rest[: len(slots)], rest[len(slots) :]
    width = chunks[0].shape[1]
    place(chunks, slots, me_ref, hidden_ref, both_ref, 0)
    p_ref[...] = base_ref[...] + p_term(q_ref[...], both_ref[:, :width], both_ref[:, width:])


def late_part(me, q, hidden, base, chunks, slots):
    cap, width = chunks[0].shape
    ff = hidden.shape[1]
    return call(
        functools.partial(late_kernel, slots),
        "late_rows",
        (me,),
        (q, hidden, base, *chunks),
        [((q.shape[0], ff), F32), ((cap * len(slots), width + ff), BF16)],
        flops=10**6,
        nbytes=10**4,
    )


def slot_kernel(at, count, both_ref, weight_ref, *rest):
    outs = rest[len(rest) - count :]
    cap, width = outs[0].shape[0], weight_ref.shape[1]
    res = dot_nt(both_ref[at : at + cap * count, :width], weight_ref[...]).astype(BF16)
    for k, out in enumerate(outs):
        out[...] = res[k * cap : (k + 1) * cap]


def slot_grads(both, weight, before, at, cap, count, flops):
    return call(
        functools.partial(slot_kernel, at, count),
        "slot_grads",
        (),
        (both, weight, *before),
        [((cap, weight.shape[0]), BF16)] * count,
        flops=flops,
        nbytes=10**4,
    )


def s_columns(part, p3, ys, error_ref, groups, out_ref):
    half = out_ref.shape[1]
    for j in range(0, half, COLS):
        cols = pl.ds(pl.multiple_of(part * half + j, COLS), COLS)
        res = dot_nn(p3, error_ref[:, cols])
        for y, group in zip(ys, groups):
            res = res + dot_nn(y, group[:, cols])
        out_ref[:, j : j + COLS] = fold3(res)


def s_send_kernel(count, core_ref, pa_ref, pb_ref, error_ref, *rest):
    groups = rest[:count]
    p_out, send_ref, p3_ref, *y_refs = rest[count:]
    total = pa_ref[...] + pb_ref[...]
    p_out[...] = total
    p3_ref[...] = stack3(total)
    width = error_ref.shape[1]
    for y_ref, group in zip(y_refs, groups):
        y_ref[...] = stack3(fold3(dot_nt(p3_ref[...], group[:, width:])))
    s_columns(1 - core_ref[0], p3_ref[...], [y[...] for y in y_refs], error_ref, groups, send_ref)


def s_send(core, pa, pb, error, groups):
    rank, ff = pa.shape
    width = error.shape[1]
    return call(
        functools.partial(s_send_kernel, len(groups)),
        "s_send",
        (core,),
        (pa, pb, error, *groups),
        [((rank, ff), F32), ((rank, width // 2), F32), ((3 * rank, ff), BF16)]
        + [((3 * rank, group.shape[0]), BF16) for group in groups],
        nbytes=7 * 10**6,
    )


def s_keep_kernel(count, core_ref, p3_ref, error_ref, *rest):
    ys, groups, (keep_ref, token_ref) = rest[:count], rest[count : 2 * count], rest[2 * count :]
    set_token(token_ref)
    s_columns(core_ref[0], p3_ref[...], [y[...] for y in ys], error_ref, groups, keep_ref)


def s_keep(core, p3, ys, error, groups):
    rank = p3.shape[0] // 3
    return call(
        functools.partial(s_keep_kernel, len(groups)),
        "s_keep",
        (core,),
        (p3, error, *ys, *groups),
        [((rank, error.shape[1] // 2), F32), TOKEN],
        nbytes=7 * 10**6,
    )


def basis_kernel(p_ref, before_ref, basis_ref, linv_ref, left_ref):
    p = p_ref[...]
    rank = p.shape[0]
    p3 = stack3(p)
    gram_rows = fold3(dot_nt(p3, p3))
    gram = gram_rows[:, :rank] + (gram_rows[:, rank : 2 * rank] + gram_rows[:, 2 * rank :])
    row = lax.broadcasted_iota(jnp.int32, (rank, rank), 0)
    col = lax.broadcasted_iota(jnp.int32, (rank, rank), 1)
    eye = jnp.where(row == col, 1.0, 0.0)
    aug = jnp.concatenate([gram, eye], axis=1)
    sub, group = 8, 4
    shape = (sub, 2 * rank)
    blocks = [aug[b * sub : (b + 1) * sub] for b in range(rank // sub)]
    sub_id = lax.broadcasted_iota(jnp.int32, shape, 0)
    for k in range(0, rank, group):
        kb, kr = divmod(k, sub)
        spread = {
            (b, i): jnp.broadcast_to(blocks[b][:, k + i : k + i + 1], shape)
            for b in range(kb, rank // sub)
            for i in range(group)
        }
        low, scale, pivots = {}, [], []
        for i in range(group):
            for j in range(i + 1):
                left = jnp.broadcast_to(spread[kb, j][kr + i : kr + i + 1], shape)
                for m in range(j):
                    left = left - low[i, m] * low[j, m]
                low[i, j] = left * scale[j] if j < i else left
            scale.append(lax.rsqrt(low[i, i]))
            pivot = jnp.broadcast_to(blocks[kb][kr + i : kr + i + 1], shape)
            for m in range(i):
                pivot = pivot - low[i, m] * pivots[m]
            pivots.append(pivot * scale[i])
        for b in range(kb, rank // sub):
            updated, factors = blocks[b], []
            for i in range(group):
                factor = spread[b, i]
                for m in range(i):
                    factor = factor - factors[m] * low[i, m]
                factors.append(factor * scale[i])
                updated = updated - factors[i] * pivots[i]
            if b == kb:
                updated = jnp.where(sub_id >= kr + group, updated, blocks[b])
                for i in range(group):
                    updated = jnp.where(sub_id == kr + i, pivots[i], updated)
            blocks[b] = updated
    linv = jnp.concatenate(blocks, axis=0)[:, rank:]
    linv_ref[...] = linv
    basis = full_dot(linv, p)
    basis_ref[...] = basis
    hi, mid, lo = split3(basis)
    left_ref[...] = jnp.concatenate([hi, hi, mid, mid, hi, lo], axis=0).T


def basis_of(p, before):
    rank, ff = p.shape
    return call(
        basis_kernel,
        "basis",
        (),
        (p, before),
        [((rank, ff), F32), ((rank, rank), F32), ((ff, 6 * rank), BF16)],
        flops=10**10,
    )


def moment_kernel(before_ref, moment_ref, both_ref, out_ref):
    width = out_ref.shape[1]
    hidden_t = both_ref[:, width:].T
    for j in range(0, width, COLS):
        cols = slice(j, j + COLS)
        out_ref[:, cols] = moment_ref[:, cols] + dot_nn(hidden_t, both_ref[:, cols])


def moment_add(before, moment, both):
    return call(
        moment_kernel,
        "moment_add",
        (),
        (before, moment, both),
        [(moment.shape, F32)],
        flops=10**10,
    )[0]


def q_kernel(replicas, mine_ref, far_ref, linv_ref, out_ref):
    out_ref[...] = full_dot(linv_ref[...], mine_ref[...] + far_ref[...]) * (1.0 / replicas)


def q_half(mine, far, linv, replicas):
    return call(functools.partial(q_kernel, replicas), "q_half", (), (mine, far, linv), [(mine.shape, F32)])[0]


def error_block(part, k, block, q_ref, left_ref, moment_ref, right):
    rank, half = q_ref.shape
    here = pl.ds(k * block, block)
    cols = pl.ds(pl.multiple_of(part * half + k * block, block), block)
    hi, mid, lo = split3(-q_ref[:, here])
    for i, piece in enumerate((hi, mid, hi, mid, lo, hi)):
        right[i * rank : (i + 1) * rank, here] = piece
    return (moment_ref[:, cols] + dot_nn(left_ref[...], right[:, here])).astype(BF16)


def error_first_kernel(block, core_ref, q_ref, left_ref, moment_ref, out_ref, right):
    for k in range(q_ref.shape[1] // block):
        here = pl.ds(k * block, block)
        out_ref[:, here] = error_block(core_ref[0], k, block, q_ref, left_ref, moment_ref, right)


def error_first(core, q, left, moment):
    half = q.shape[1]
    return call(
        functools.partial(error_first_kernel, 256),
        "new_error_first",
        (core,),
        (q, left, moment),
        [((moment.shape[0], half), BF16)],
        [pltpu.VMEM((left.shape[1], half), BF16)],
        flops=10**10,
    )[0]


def last_kernel(block, parts, core_ref, mine_ref, other_ref, left_ref, moment_ref, first_ref, *rest):
    count = len(rest) - (10 if parts else 5)
    chunks = rest[2 : 2 + count] if parts else ()
    near_ref, pick_ref = rest[:2] if parts else (None, None)
    outs = rest[2 + count :] if parts else rest
    q_hbm, out_hbm = outs[:2]
    right, held, sems = outs[-3:]
    half = mine_ref.shape[1]
    part = 1 - core_ref[0]
    at_mine = pl.ds(pl.multiple_of(core_ref[0] * half, half), half)
    at_other = pl.ds(pl.multiple_of(part * half, half), half)
    copies = [
        pltpu.make_async_copy(first_ref, out_hbm.at[:, at_mine], sems.at[0]),
        pltpu.make_async_copy(mine_ref, q_hbm.at[:, at_mine], sems.at[1]),
        pltpu.make_async_copy(other_ref, q_hbm.at[:, at_other], sems.at[2]),
    ]
    for copy in copies:
        copy.start()
    steps = half // block
    for k in range(steps):
        here = pl.ds(k * block, block)
        cols = pl.ds(pl.multiple_of(part * half + k * block, block), block)
        held[:, here] = error_block(part, k, block, other_ref, left_ref, moment_ref, right)
        copies.append(pltpu.make_async_copy(held.at[:, here], out_hbm.at[:, cols], sems.at[3 + k]))
        copies[-1].start()
    if parts:
        grad_hbm, cat, grad_ref = outs[2:5]
        cap = chunks[0].shape[0]
        for k in range(count):
            cat[k * cap : (k + 1) * cap, :] = chunks[k][...]
        rows = grad_ref.shape[0] // parts
        for k in range(parts):
            at = pl.ds(k * rows, rows)
            grad_ref[at, :] = near_ref[at, :] + dot_nn(pick_ref[at, :], cat[...]).astype(BF16)
            copies.append(pltpu.make_async_copy(grad_ref.at[at, :], grad_hbm.at[at, :], sems.at[3 + steps + k]))
            copies[-1].start()
    for copy in copies:
        copy.wait()


def last_part(core, mine, other, left, moment, first, near=None, pick=None, chunks=()):
    ff, width = moment.shape
    rank, half = mine.shape
    block = 256
    parts = 2 if chunks else 0
    operands = [mine, other, left, moment, first]
    outs = [((rank, width), F32), ((ff, width), BF16)]
    scratch = []
    if chunks:
        operands += [near, pick, *chunks]
        outs.append((near.shape, BF16))
        scratch = [pltpu.VMEM((pick.shape[1], ff), BF16), pltpu.VMEM(near.shape, BF16)]
    scratch += [
        pltpu.VMEM((left.shape[1], half), BF16),
        pltpu.VMEM((ff, half), BF16),
        pltpu.SemaphoreType.DMA((3 + half // block + parts,)),
    ]
    return call(
        functools.partial(last_kernel, block, parts),
        "new_error_last",
        (core,),
        operands,
        outs,
        scratch,
        out_specs=[in_hbm()] * len(outs),
        flops=10**10,
    )


def pick_kernel(n, cap, masks, me_ref, counts_ref, order_ref, out_ref, held):
    order = order_ref[...]
    j = lax.broadcasted_iota(jnp.int32, (cap, order.shape[1]), 0)
    for k, mask in enumerate(masks):
        expert = me_ref[0] ^ mask
        start = jnp.int32(0)
        for e in range(n):
            start = start + jnp.where(e < expert, counts_ref[e], 0)
        hit = (order == j + start) & (j < counts_ref[expert])
        held[k * cap : (k + 1) * cap, :] = jnp.where(hit, 1.0, 0.0)
    out_ref[...] = held[...].T.astype(BF16)


def pick_of(me, counts, order, n, cap, masks):
    tokens = order.shape[1]
    slots = len(masks) * cap
    return call(
        functools.partial(pick_kernel, n, cap, masks),
        "pick_rows",
        (me, counts),
        (order,),
        [((tokens, slots), BF16)],
        [pltpu.VMEM((slots, tokens), F32)],
        flops=10**6,
        nbytes=10**4,
    )[0]


def unpack_first_kernel(count, before_ref, pick_ref, *rest):
    chunks, (out_ref, token_ref, cat) = rest[:count], rest[count:]
    cap = chunks[0].shape[0]
    for k in range(count):
        cat[k * cap : (k + 1) * cap, :] = chunks[k][...]
    out_ref[...] = dot_nn(pick_ref[...], cat[...]).astype(BF16)
    set_token(token_ref)


def unpack_first(before, pick, chunks):
    cap, ff = chunks[0].shape
    return call(
        functools.partial(unpack_first_kernel, len(chunks)),
        "unpack_first",
        (),
        (before, pick, *chunks),
        [((pick.shape[0], ff), BF16), TOKEN],
        [pltpu.VMEM((len(chunks) * cap, ff), BF16)],
        flops=10**10,
    )


def pack_plain(route_count, local_rows, experts, capacity):
    total_rows, width = local_rows.shape
    route_starts = jnp.cumsum(route_count) - route_count
    slot_ids = jnp.arange(capacity, dtype=jnp.int32)
    pick_index = jnp.minimum(route_starts[:, None] + slot_ids[None, :], total_rows - 1)
    slot_valid = slot_ids[None, :] < route_count[:, None]
    outgoing = local_rows[pick_index.reshape(-1)].reshape(experts, capacity, width)
    return jnp.where(slot_valid[:, :, None], outgoing, jnp.zeros((), BF16))


def unpack_plain(route_count, order_local, returned, experts, capacity):
    route_ends = jnp.cumsum(route_count)
    route_starts = route_ends - route_count
    expert_of = jnp.sum((route_ends[None, :] <= order_local[:, None]).astype(jnp.int32), axis=1)
    row_base = jnp.arange(experts, dtype=jnp.int32) * capacity - route_starts
    return returned[row_base[expert_of] + order_local]


def add_kernel(a_ref, b_ref, *rest):
    rest[-1][...] = a_ref[...] + b_ref[...]


def add(a, b, *before):
    return call(add_kernel, "add", (), (a, b, *before), [(a.shape, F32)], limit=4, flops=10**6)[0]


def pass_kernel(x_ref, before_ref, out_ref):
    out_ref[...] = x_ref[...]


def pass_on(x, before):
    return call(pass_kernel, "pass_on", (), (x, before), [(x.shape, x.dtype)], limit=4, flops=10**6)[0]


def shards(n_expert, n_dp, grad_rows, counts, order, hidden, down_weight, error_in, q_init):
    rows = grad_rows[0]
    count = counts[0, 0]
    saved = hidden[0, 0]
    weight = down_weight[0]
    error = error_in[0, 0]
    q = q_init[0].T
    ff = saved.shape[1]
    capacity = saved.shape[0] // n_expert
    me = lax.axis_index("expert").astype(jnp.int32)[None]
    core = (lax.axis_index("dp").astype(jnp.int32) & 1)[None]
    core_pairs = [(d, d ^ 1) for d in range(n_dp)]
    chip_pairs = [(d, d ^ 2) for d in range(n_dp)]
    by_pairs = n_expert == 8 and capacity % ROW_TILE == 0

    if by_pairs:
        far = tuple(reversed(range(n_expert // 2, n_expert)))
        near = tuple(reversed(range(0, n_expert // 2)))
        first, last = far[:1] + near, far[1:]

        def swap(x, mask):
            return lax.ppermute(x, "expert", [(e, e ^ mask) for e in range(n_expert)])

        others = far[1:] + near
        packed = {far[0]: pack(me, core, counts[0], rows, n_expert, capacity, far[:1], 4 * 10**6, whole_vmem(), 62)[0]}
        packed.update(zip(others, pack(me, core, counts[0], rows, n_expert, capacity, others, 10**4, in_hbm(), FULL)))
        arrived = {m: swap(packed[m], m) if m else packed[m] for m in far + near}
        pick_near = pick_of(me, count, order, n_expert, capacity, near)
        pick_far = pick_of(me, count, order, n_expert, capacity, far)
        p_first, both_first, moment, *back = early_part(
            me, q, saved, error, weight, [arrived[m] for m in first], first
        )
        back_near = [swap(x, m) if m else x for x, m in zip(back[1:], near)]
        p_mine, both_last = late_part(me, q, saved, p_first, [arrived[m] for m in last], last)
        back_next = slot_grads(
            both_last, weight, (pick_near, pick_far, *back_near), 0, capacity, len(last), 10**10
        )
        back_soon = pass_on(back[0], back_next[0])
        before, groups = back_next[:1], [both_first, both_last]
    else:
        outgoing = pack_plain(count, rows, n_expert, capacity)
        arrived = lax.all_to_all(outgoing, "expert", split_axis=0, concat_axis=0, tiled=True)
        arrived = arrived.reshape(n_expert * capacity, rows.shape[1])
        p_mine, both_first, moment, back = early_part(me, q, saved, error, weight, [arrived], (None,))
        before, groups = [], [both_first]
        back = back.reshape(n_expert, capacity, ff)
        returned = lax.all_to_all(back, "expert", split_axis=0, concat_axis=0, tiled=True)
        returned = returned.reshape(n_expert * capacity, ff)
    p_chip = add(p_mine, lax.ppermute(p_mine, "dp", core_pairs), *before)
    p_far = lax.ppermute(p_chip, "dp", chip_pairs)
    if by_pairs:
        back_sent = [pass_on(x, p_chip) for x in back_next[:-1]]
        moment = moment_add(back_sent[-1], moment, both_last)
    p_total, s_sent, p3, *ys = s_send(core, p_chip, p_far, error, groups)
    s_swapped = lax.ppermute(s_sent, "dp", core_pairs)
    s_kept, token = s_keep(core, p3, ys, error, groups)
    if by_pairs:
        grad_near, token = unpack_first(token, pick_near, back_near)
    s_half = add(s_kept, s_swapped, token)
    if by_pairs:
        back_last = pass_on(back_next[-1], s_half)
        back_far = [swap(x, m) for x, m in zip([back_soon, *back_sent, back_last], far)]
    basis, linv, left = basis_of(p_total, back_last if by_pairs else p_total)
    q_mine = q_half(s_half, lax.ppermute(s_half, "dp", chip_pairs), linv, n_dp)
    q_other = lax.ppermute(q_mine, "dp", core_pairs)
    first_half = error_first(core, q_mine, left, moment)
    if by_pairs:
        q_factor, error_out, input_grad = last_part(
            core, q_mine, q_other, left, moment, first_half, grad_near, pick_far, back_far
        )
    else:
        q_factor, error_out = last_part(core, q_mine, q_other, left, moment, first_half)
        input_grad = unpack_plain(count, order[0], returned, n_expert, capacity)
    return (input_grad[None], basis.T[None], q_factor.T[None], error_out[None, None])


def solution(mesh):
    placed = (
        P("dp", "expert", None),
        P("dp", "expert", None),
        P("dp", "expert"),
        P("dp", "expert", None, None),
        P("expert", None, None),
        P("dp", "expert", None, None),
        P("expert", None, None),
    )
    return jax.shard_map(
        functools.partial(shards, mesh.shape["expert"], mesh.shape["dp"]),
        mesh=mesh,
        in_specs=placed,
        out_specs=(
            P("dp", "expert", None),
            P("expert", None, None),
            P("expert", None, None),
            P("dp", "expert", None, None),
        ),
        check_vma=False,
    )
```

```python
import functools

import jax
import jax.numpy as jnp
from jax import lax
from jax.experimental import pallas as pl
from jax.experimental.pallas import tpu as pltpu
from jax.sharding import PartitionSpec as P

F32 = jnp.float32
BF16 = jnp.bfloat16
ROW_TILE = 16
COLS = 512
MIB = 1024 * 1024
FULL = 58


def whole_vmem():
    return pl.BlockSpec(memory_space=pltpu.VMEM)


def split3(x):
    hi = x.astype(BF16)
    rest = x - hi.astype(F32)
    mid = rest.astype(BF16)
    lo = (rest - mid.astype(F32)).astype(BF16)
    return hi, mid, lo


def stack3(x):
    return jnp.concatenate(split3(x), axis=0)


def fold3(x):
    n = x.shape[0] // 3
    return x[:n] + (x[n : 2 * n] + x[2 * n :])


def dot_nt(a, b):
    return lax.dot_general(a, b, (((1,), (1,)), ((), ())), preferred_element_type=F32)


def dot_nn(a, b):
    return jnp.dot(a, b, preferred_element_type=F32)


def full_dot(a, b):
    return jnp.dot(a, b, precision=lax.Precision.HIGHEST, preferred_element_type=F32)

def in_hbm():
    return pl.BlockSpec(memory_space=pltpu.HBM)


TOKEN = ((8, 128), F32)


def set_token(ref):
    ref[...] = jnp.zeros(ref.shape, ref.dtype)


def cost(flops, nbytes):
    return pl.CostEstimate(flops=flops, bytes_accessed=nbytes, transcendentals=0)


def call(kernel, name, scalars, operands, outs, scratch=(), limit=12, flops=10**9, nbytes=10**6, specs=None, out_specs=None):
    outs = [jax.ShapeDtypeStruct(shape, dtype) for shape, dtype in outs]
    return pl.pallas_call(
        kernel,
        grid_spec=pltpu.PrefetchScalarGridSpec(
            num_scalar_prefetch=len(scalars),
            grid=(),
            in_specs=specs or [whole_vmem()] * len(operands),
            out_specs=out_specs or [whole_vmem()] * len(outs),
            scratch_shapes=list(scratch),
        ),
        out_shape=outs,
        compiler_params=pltpu.CompilerParams(vmem_limit_bytes=limit * MIB),
        cost_estimate=cost(flops, nbytes),
        name=name,
    )(*scalars, *operands)


def start_of(counts_ref, expert, n):
    start = jnp.int32(0)
    for e in range(n):
        start = start + jnp.where(e < expert, counts_ref[0, e], 0)
    return start


def pack_first_kernel(n, mask, me_ref, core_ref, counts_hbm, rows_hbm, out_ref, counts_ref, rows_ref, sems):
    cap = out_ref.shape[0]
    total, window = rows_hbm.shape[0], rows_ref.shape[0]
    dest = me_ref[0] ^ mask
    base = jnp.clip(total - cap * (n - dest), 0, total - window)
    base = pl.multiple_of(base, ROW_TILE)
    copy_counts = pltpu.make_async_copy(counts_hbm, counts_ref, sems.at[0])
    copy_rows = pltpu.make_async_copy(rows_hbm.at[pl.ds(base, window), :], rows_ref, sems.at[1])
    copy_counts.start()
    copy_rows.start()
    copy_counts.wait()
    j = lax.broadcasted_iota(jnp.int32, (cap, window), 0)
    w = lax.broadcasted_iota(jnp.int32, (cap, window), 1)
    hit = (w == j + (start_of(counts_ref, dest, n) - base)) & (j < counts_ref[0, dest])
    pick = jnp.where(hit, 1.0, 0.0).astype(BF16)
    copy_rows.wait()
    out_ref[...] = dot_nn(pick, rows_ref[...]).astype(BF16)


def pack_first(me, core, counts, rows, n, cap, mask):
    total, width = rows.shape
    window = min(total, cap * (n + 1) - total)
    return call(
        functools.partial(pack_first_kernel, n, mask),
        "pack_first",
        (me, core),
        (counts, rows),
        [((cap, width), BF16)],
        [pltpu.SMEM(counts.shape, jnp.int32), pltpu.VMEM((window, width), BF16), pltpu.SemaphoreType.DMA((2,))],
        specs=[in_hbm()] * 2,
        limit=62,
        flops=10**6,
        nbytes=4 * 10**6,
    )[0]


def pack_kernel(n, cap, masks, me_ref, counts_hbm, rows_hbm, *rest):
    outs = rest[: len(masks)]
    counts_ref, rows_ref, held, sems, out_sems = rest[len(masks) :]
    total = rows_ref.shape[0]
    window = -(-(cap + ROW_TILE - 1) // ROW_TILE) * ROW_TILE
    copy_counts = pltpu.make_async_copy(counts_hbm, counts_ref, sems.at[0])
    copy_rows = pltpu.make_async_copy(rows_hbm, rows_ref, sems.at[1])
    copy_counts.start()
    copy_rows.start()
    copy_counts.wait()
    j = lax.broadcasted_iota(jnp.int32, (cap, window), 0)
    w = lax.broadcasted_iota(jnp.int32, (cap, window), 1)
    bases, picks = [], []
    for mask in masks:
        dest = me_ref[0] ^ mask
        start = start_of(counts_ref, dest, n)
        base = jnp.minimum((start // ROW_TILE) * ROW_TILE, total - window)
        bases.append(pl.multiple_of(base, ROW_TILE))
        hit = (w == j + (start - base)) & (j < counts_ref[0, dest])
        picks.append(jnp.where(hit, 1.0, 0.0).astype(BF16))
    copy_rows.wait()
    copies = []
    for k, (base, pick) in enumerate(zip(bases, picks)):
        held[k] = dot_nn(pick, rows_ref[pl.ds(base, window), :]).astype(BF16)
        copies.append(pltpu.make_async_copy(held.at[k], outs[k], out_sems.at[k]))
        copies[k].start()
    for copy in copies:
        copy.wait()


def pack(me, counts, rows, n, cap, masks):
    count, width = len(masks), rows.shape[1]
    return call(
        functools.partial(pack_kernel, n, cap, masks),
        "pack_rows",
        (me,),
        (counts, rows),
        [((cap, width), BF16)] * count,
        [
            pltpu.SMEM(counts.shape, jnp.int32),
            pltpu.VMEM(rows.shape, BF16),
            pltpu.VMEM((count, cap, width), BF16),
            pltpu.SemaphoreType.DMA((2,)),
            pltpu.SemaphoreType.DMA((count,)),
        ],
        specs=[in_hbm()] * 2,
        out_specs=[in_hbm()] * count,
        limit=FULL,
        flops=10**6,
        nbytes=10**4,
    )


def source_at(me_ref, slot, cap):
    if slot is None:
        return 0
    return pl.multiple_of((me_ref[0] ^ slot) * cap, ROW_TILE)


def place(chunks, slots, me_ref, hidden_ref, both_ref, at):
    cap, width = chunks[0].shape
    for k, slot in enumerate(slots):
        rows = pl.ds(at + k * cap, cap)
        both_ref[rows, :width] = chunks[k][...]
        both_ref[rows, width:] = hidden_ref[pl.ds(source_at(me_ref, slot, cap), cap), :]


def p_term(q, rows, hidden):
    return fold3(dot_nn(stack3(dot_nt(q, rows)), hidden))


def early_kernel(slots, me_ref, q_ref, hidden_ref, error_ref, weight_ref, *rest):
    chunks = rest[: len(slots)]
    p_ref, both_ref, moment_ref, *slot_refs = rest[len(slots) :]
    cap = chunks[0].shape[0]
    width = error_ref.shape[1]
    place(chunks, slots, me_ref, hidden_ref, both_ref, 0)
    q = q_ref[...]
    p_ref[...] = dot_nt(q, error_ref[...]) + p_term(q, both_ref[:, :width], both_ref[:, width:])
    hidden_t = both_ref[:, width:].T
    for j in range(0, width, COLS):
        block = dot_nn(hidden_t, both_ref[:, j : j + COLS])
        moment_ref[:, j : j + COLS] = error_ref[:, j : j + COLS].astype(F32) + block
    res = dot_nt(both_ref[:, :width], weight_ref[...]).astype(BF16)
    for k, ref in enumerate(slot_refs):
        ref[...] = res[k * cap : (k + 1) * cap]


def early_part(me, q, hidden, error, weight, chunks, slots):
    cap, width = chunks[0].shape
    ff = hidden.shape[1]
    rows = cap * len(slots)
    return call(
        functools.partial(early_kernel, slots),
        "early_rows",
        (me,),
        (q, hidden, error, weight, *chunks),
        [((q.shape[0], ff), F32), ((rows, width + ff), BF16), ((ff, width), F32)]
        + [((cap, ff), BF16)] * len(slots),
        flops=2 * 10**9,
        nbytes=10**7,
    )


def late_kernel(slots, me_ref, q_ref, hidden_ref, base_ref, *rest):
    chunks, (p_ref, both_ref) = rest[: len(slots)], rest[len(slots) :]
    width = chunks[0].shape[1]
    place(chunks, slots, me_ref, hidden_ref, both_ref, 0)
    p_ref[...] = base_ref[...] + p_term(q_ref[...], both_ref[:, :width], both_ref[:, width:])


def late_part(me, q, hidden, base, chunks, slots):
    cap, width = chunks[0].shape
    ff = hidden.shape[1]
    return call(
        functools.partial(late_kernel, slots),
        "late_rows",
        (me,),
        (q, hidden, base, *chunks),
        [((q.shape[0], ff), F32), ((cap * len(slots), width + ff), BF16)],
        flops=10**6,
        nbytes=10**4,
    )


def slot_kernel(at, count, both_ref, weight_ref, *rest):
    outs = rest[len(rest) - count :]
    cap, width = outs[0].shape[0], weight_ref.shape[1]
    res = dot_nt(both_ref[at : at + cap * count, :width], weight_ref[...]).astype(BF16)
    for k, out in enumerate(outs):
        out[...] = res[k * cap : (k + 1) * cap]


def slot_grads(both, weight, before, at, cap, count, flops):
    return call(
        functools.partial(slot_kernel, at, count),
        "slot_grads",
        (),
        (both, weight, *before),
        [((cap, weight.shape[0]), BF16)] * count,
        flops=flops,
        nbytes=10**4,
    )


def s_columns(part, p3, ys, error_ref, groups, out_ref):
    half = out_ref.shape[1]
    for j in range(0, half, COLS):
        cols = pl.ds(pl.multiple_of(part * half + j, COLS), COLS)
        res = dot_nn(p3, error_ref[:, cols])
        for y, group in zip(ys, groups):
            res = res + dot_nn(y, group[:, cols])
        out_ref[:, j : j + COLS] = fold3(res)


def s_send_kernel(count, core_ref, pa_ref, pb_ref, error_ref, *rest):
    groups = rest[:count]
    p_out, send_ref, p3_ref, *y_refs = rest[count:]
    total = pa_ref[...] + pb_ref[...]
    p_out[...] = total
    p3_ref[...] = stack3(total)
    width = error_ref.shape[1]
    for y_ref, group in zip(y_refs, groups):
        y_ref[...] = stack3(fold3(dot_nt(p3_ref[...], group[:, width:])))
    s_columns(1 - core_ref[0], p3_ref[...], [y[...] for y in y_refs], error_ref, groups, send_ref)


def s_send(core, pa, pb, error, groups):
    rank, ff = pa.shape
    width = error.shape[1]
    return call(
        functools.partial(s_send_kernel, len(groups)),
        "s_send",
        (core,),
        (pa, pb, error, *groups),
        [((rank, ff), F32), ((rank, width // 2), F32), ((3 * rank, ff), BF16)]
        + [((3 * rank, group.shape[0]), BF16) for group in groups],
        nbytes=7 * 10**6,
    )


def s_keep_kernel(count, core_ref, p3_ref, error_ref, *rest):
    ys, groups, (keep_ref, token_ref) = rest[:count], rest[count : 2 * count], rest[2 * count :]
    set_token(token_ref)
    s_columns(core_ref[0], p3_ref[...], [y[...] for y in ys], error_ref, groups, keep_ref)


def s_keep(core, p3, ys, error, groups):
    rank = p3.shape[0] // 3
    return call(
        functools.partial(s_keep_kernel, len(groups)),
        "s_keep",
        (core,),
        (p3, error, *ys, *groups),
        [((rank, error.shape[1] // 2), F32), TOKEN],
        nbytes=7 * 10**6,
    )


def basis_kernel(p_ref, before_ref, basis_ref, linv_ref, left_ref):
    p = p_ref[...]
    rank = p.shape[0]
    p3 = stack3(p)
    gram_rows = fold3(dot_nt(p3, p3))
    gram = gram_rows[:, :rank] + (gram_rows[:, rank : 2 * rank] + gram_rows[:, 2 * rank :])
    row = lax.broadcasted_iota(jnp.int32, (rank, rank), 0)
    col = lax.broadcasted_iota(jnp.int32, (rank, rank), 1)
    eye = jnp.where(row == col, 1.0, 0.0)
    aug = jnp.concatenate([gram, eye], axis=1)
    sub, group = 8, 4
    shape = (sub, 2 * rank)
    blocks = [aug[b * sub : (b + 1) * sub] for b in range(rank // sub)]
    sub_id = lax.broadcasted_iota(jnp.int32, shape, 0)
    for k in range(0, rank, group):
        kb, kr = divmod(k, sub)
        spread = {
            (b, i): jnp.broadcast_to(blocks[b][:, k + i : k + i + 1], shape)
            for b in range(kb, rank // sub)
            for i in range(group)
        }
        low, scale, pivots = {}, [], []
        for i in range(group):
            for j in range(i + 1):
                left = jnp.broadcast_to(spread[kb, j][kr + i : kr + i + 1], shape)
                for m in range(j):
                    left = left - low[i, m] * low[j, m]
                low[i, j] = left * scale[j] if j < i else left
            scale.append(lax.rsqrt(low[i, i]))
            pivot = jnp.broadcast_to(blocks[kb][kr + i : kr + i + 1], shape)
            for m in range(i):
                pivot = pivot - low[i, m] * pivots[m]
            pivots.append(pivot * scale[i])
        for b in range(kb, rank // sub):
            updated, factors = blocks[b], []
            for i in range(group):
                factor = spread[b, i]
                for m in range(i):
                    factor = factor - factors[m] * low[i, m]
                factors.append(factor * scale[i])
                updated = updated - factors[i] * pivots[i]
            if b == kb:
                updated = jnp.where(sub_id >= kr + group, updated, blocks[b])
                for i in range(group):
                    updated = jnp.where(sub_id == kr + i, pivots[i], updated)
            blocks[b] = updated
    linv = jnp.concatenate(blocks, axis=0)[:, rank:]
    linv_ref[...] = linv
    basis = full_dot(linv, p)
    basis_ref[...] = basis
    hi, mid, lo = split3(basis)
    left_ref[...] = jnp.concatenate([hi, hi, mid, mid, hi, lo], axis=0).T


def basis_of(p, before):
    rank, ff = p.shape
    return call(
        basis_kernel,
        "basis",
        (),
        (p, before),
        [((rank, ff), F32), ((rank, rank), F32), ((ff, 6 * rank), BF16)],
        flops=10**10,
    )


def moment_kernel(before_ref, moment_ref, both_ref, out_ref):
    width = out_ref.shape[1]
    hidden_t = both_ref[:, width:].T
    for j in range(0, width, COLS):
        cols = slice(j, j + COLS)
        out_ref[:, cols] = moment_ref[:, cols] + dot_nn(hidden_t, both_ref[:, cols])


def moment_add(before, moment, both):
    return call(
        moment_kernel,
        "moment_add",
        (),
        (before, moment, both),
        [(moment.shape, F32)],
        nbytes=10**7,
    )[0]


def q_kernel(replicas, mine_ref, far_ref, linv_ref, out_ref):
    out_ref[...] = full_dot(linv_ref[...], mine_ref[...] + far_ref[...]) * (1.0 / replicas)


def q_half(mine, far, linv, replicas):
    return call(functools.partial(q_kernel, replicas), "q_half", (), (mine, far, linv), [(mine.shape, F32)])[0]


def error_block(part, k, block, q_ref, left_ref, moment_ref, right):
    rank, half = q_ref.shape
    here = pl.ds(k * block, block)
    cols = pl.ds(pl.multiple_of(part * half + k * block, block), block)
    hi, mid, lo = split3(-q_ref[:, here])
    for i, piece in enumerate((hi, mid, hi, mid, lo, hi)):
        right[i * rank : (i + 1) * rank, here] = piece
    return (moment_ref[:, cols] + dot_nn(left_ref[...], right[:, here])).astype(BF16)


def error_first_kernel(block, core_ref, q_ref, left_ref, moment_ref, out_ref, right):
    for k in range(q_ref.shape[1] // block):
        here = pl.ds(k * block, block)
        out_ref[:, here] = error_block(core_ref[0], k, block, q_ref, left_ref, moment_ref, right)


def error_first(core, q, left, moment):
    half = q.shape[1]
    return call(
        functools.partial(error_first_kernel, 256),
        "new_error_first",
        (core,),
        (q, left, moment),
        [((moment.shape[0], half), BF16)],
        [pltpu.VMEM((left.shape[1], half), BF16)],
        flops=10**10,
    )[0]


def error_second_kernel(block, core_ref, mine_ref, other_ref, left_ref, moment_ref, first_ref, *rest):
    q_hbm, out_hbm, token_ref, right, held, sems = rest
    set_token(token_ref)
    half = mine_ref.shape[1]
    part = 1 - core_ref[0]
    at_mine = pl.ds(pl.multiple_of(core_ref[0] * half, half), half)
    at_other = pl.ds(pl.multiple_of(part * half, half), half)
    copies = [
        pltpu.make_async_copy(first_ref, out_hbm.at[:, at_mine], sems.at[0]),
        pltpu.make_async_copy(mine_ref, q_hbm.at[:, at_mine], sems.at[1]),
        pltpu.make_async_copy(other_ref, q_hbm.at[:, at_other], sems.at[2]),
    ]
    for copy in copies:
        copy.start()
    for k in range(half // block):
        here = pl.ds(k * block, block)
        cols = pl.ds(pl.multiple_of(part * half + k * block, block), block)
        held[:, here] = error_block(part, k, block, other_ref, left_ref, moment_ref, right)
        copies.append(pltpu.make_async_copy(held.at[:, here], out_hbm.at[:, cols], sems.at[3 + k]))
        copies[-1].start()
    for copy in copies:
        copy.wait()


def error_second(core, mine, other, left, moment, first):
    ff, width = moment.shape
    rank, half = mine.shape
    block = 256
    return call(
        functools.partial(error_second_kernel, block),
        "new_error_second",
        (core,),
        (mine, other, left, moment, first),
        [((rank, width), F32), ((ff, width), BF16), TOKEN],
        [
            pltpu.VMEM((left.shape[1], half), BF16),
            pltpu.VMEM((ff, half), BF16),
            pltpu.SemaphoreType.DMA((3 + half // block,)),
        ],
        out_specs=[in_hbm(), in_hbm(), whole_vmem()],
        flops=10**10,
    )


def pick_kernel(n, cap, masks, me_ref, counts_ref, order_ref, out_ref, held):
    order = order_ref[...]
    j = lax.broadcasted_iota(jnp.int32, (cap, order.shape[1]), 0)
    for k, mask in enumerate(masks):
        expert = me_ref[0] ^ mask
        start = jnp.int32(0)
        for e in range(n):
            start = start + jnp.where(e < expert, counts_ref[e], 0)
        hit = (order == j + start) & (j < counts_ref[expert])
        held[k * cap : (k + 1) * cap, :] = jnp.where(hit, 1.0, 0.0)
    out_ref[...] = held[...].T.astype(BF16)


def pick_of(me, counts, order, n, cap, masks):
    tokens = order.shape[1]
    slots = len(masks) * cap
    return call(
        functools.partial(pick_kernel, n, cap, masks),
        "pick_rows",
        (me, counts),
        (order,),
        [((tokens, slots), BF16)],
        [pltpu.VMEM((slots, tokens), F32)],
        flops=10**6,
        nbytes=10**4,
    )[0]


def unpack_first_kernel(count, before_ref, pick_ref, *rest):
    chunks, (out_ref, token_ref, cat) = rest[:count], rest[count:]
    cap = chunks[0].shape[0]
    for k in range(count):
        cat[k * cap : (k + 1) * cap, :] = chunks[k][...]
    out_ref[...] = dot_nn(pick_ref[...], cat[...]).astype(BF16)
    set_token(token_ref)


def unpack_first(before, pick, chunks):
    cap, ff = chunks[0].shape
    return call(
        functools.partial(unpack_first_kernel, len(chunks)),
        "unpack_first",
        (),
        (before, pick, *chunks),
        [((pick.shape[0], ff), BF16), TOKEN],
        [pltpu.VMEM((len(chunks) * cap, ff), BF16)],
        flops=10**10,
    )


def unpack_kernel(count, parts, token_ref, pick_ref, first_ref, *rest):
    chunks, (out_hbm, cat, out_ref, sems) = rest[:count], rest[count:]
    cap = chunks[0].shape[0]
    for k in range(count):
        cat[k * cap : (k + 1) * cap, :] = chunks[k][...]
    rows = out_ref.shape[0] // parts
    copies = []
    for k in range(parts):
        at = pl.ds(k * rows, rows)
        out_ref[at, :] = first_ref[at, :] + dot_nn(pick_ref[at, :], cat[...]).astype(BF16)
        copies.append(pltpu.make_async_copy(out_ref.at[at, :], out_hbm.at[at, :], sems.at[k]))
        copies[k].start()
    for copy in copies:
        copy.wait()


def unpack(token, pick, first, chunks):
    cap, ff = chunks[0].shape
    tokens, slots = pick.shape
    parts = 2
    return pl.pallas_call(
        functools.partial(unpack_kernel, len(chunks), parts),
        in_specs=[whole_vmem()] * (3 + len(chunks)),
        out_specs=in_hbm(),
        out_shape=jax.ShapeDtypeStruct((tokens, ff), BF16),
        scratch_shapes=[
            pltpu.VMEM((slots, ff), BF16),
            pltpu.VMEM((tokens, ff), BF16),
            pltpu.SemaphoreType.DMA((parts,)),
        ],
        compiler_params=pltpu.CompilerParams(vmem_limit_bytes=8 * MIB),
        cost_estimate=cost(10**6, 10**4),
        name="unpack_rows",
    )(token, pick, first, *chunks)


def pack_plain(route_count, local_rows, experts, capacity):
    total_rows, width = local_rows.shape
    route_starts = jnp.cumsum(route_count) - route_count
    slot_ids = jnp.arange(capacity, dtype=jnp.int32)
    pick_index = jnp.minimum(route_starts[:, None] + slot_ids[None, :], total_rows - 1)
    slot_valid = slot_ids[None, :] < route_count[:, None]
    outgoing = local_rows[pick_index.reshape(-1)].reshape(experts, capacity, width)
    return jnp.where(slot_valid[:, :, None], outgoing, jnp.zeros((), BF16))


def unpack_plain(route_count, order_local, returned, experts, capacity):
    route_ends = jnp.cumsum(route_count)
    route_starts = route_ends - route_count
    expert_of = jnp.sum((route_ends[None, :] <= order_local[:, None]).astype(jnp.int32), axis=1)
    row_base = jnp.arange(experts, dtype=jnp.int32) * capacity - route_starts
    return returned[row_base[expert_of] + order_local]


def add_kernel(a_ref, b_ref, *rest):
    rest[-1][...] = a_ref[...] + b_ref[...]


def add(a, b, *before):
    return call(add_kernel, "add", (), (a, b, *before), [(a.shape, F32)], limit=4, flops=10**6)[0]


def pass_kernel(x_ref, before_ref, out_ref):
    out_ref[...] = x_ref[...]


def pass_on(x, before):
    return call(pass_kernel, "pass_on", (), (x, before), [(x.shape, x.dtype)], limit=4, flops=10**6)[0]


def shards(n_expert, n_dp, grad_rows, counts, order, hidden, down_weight, error_in, q_init):
    rows = grad_rows[0]
    count = counts[0, 0]
    saved = hidden[0, 0]
    weight = down_weight[0]
    error = error_in[0, 0]
    q = q_init[0].T
    ff = saved.shape[1]
    capacity = saved.shape[0] // n_expert
    me = lax.axis_index("expert").astype(jnp.int32)[None]
    core = (lax.axis_index("dp").astype(jnp.int32) & 1)[None]
    core_pairs = [(d, d ^ 1) for d in range(n_dp)]
    chip_pairs = [(d, d ^ 2) for d in range(n_dp)]
    by_pairs = n_expert == 8 and capacity % ROW_TILE == 0 and rows.shape[0] % ROW_TILE == 0

    if by_pairs:
        far = tuple(reversed(range(n_expert // 2, n_expert)))
        near = tuple(reversed(range(0, n_expert // 2)))
        first, last = far[:1] + near, far[1:]

        def swap(x, mask):
            return lax.ppermute(x, "expert", [(e, e ^ mask) for e in range(n_expert)])

        others = far[1:] + near
        packed = {far[0]: pack_first(me, core, counts[0], rows, n_expert, capacity, far[0])}
        packed.update(zip(others, pack(me, counts[0], rows, n_expert, capacity, others)))
        arrived = {m: swap(packed[m], m) if m else packed[m] for m in far + near}
        pick_near = pick_of(me, count, order, n_expert, capacity, near)
        pick_far = pick_of(me, count, order, n_expert, capacity, far)
        p_first, both_first, moment, *back = early_part(
            me, q, saved, error, weight, [arrived[m] for m in first], first
        )
        back_near = [swap(x, m) if m else x for x, m in zip(back[1:], near)]
        p_mine, both_last = late_part(me, q, saved, p_first, [arrived[m] for m in last], last)
        back_next = slot_grads(
            both_last, weight, (pick_near, pick_far, *back_near), 0, capacity, len(last), 10**10
        )
        before, groups = back_next[:1], [both_first, both_last]
    else:
        outgoing = pack_plain(count, rows, n_expert, capacity)
        arrived = lax.all_to_all(outgoing, "expert", split_axis=0, concat_axis=0, tiled=True)
        arrived = arrived.reshape(n_expert * capacity, rows.shape[1])
        p_mine, both_first, moment, back = early_part(me, q, saved, error, weight, [arrived], (None,))
        before, groups = [], [both_first]
        back = back.reshape(n_expert, capacity, ff)
        returned = lax.all_to_all(back, "expert", split_axis=0, concat_axis=0, tiled=True)
        returned = returned.reshape(n_expert * capacity, ff)
    p_chip = add(p_mine, lax.ppermute(p_mine, "dp", core_pairs), *before)
    p_far = lax.ppermute(p_chip, "dp", chip_pairs)
    p_total, s_sent, p3, *ys = s_send(core, p_chip, p_far, error, groups)
    s_swapped = lax.ppermute(s_sent, "dp", core_pairs)
    s_kept, token = s_keep(core, p3, ys, error, groups)
    if by_pairs:
        grad_near, token = unpack_first(token, pick_near, back_near)
    s_half = add(s_kept, s_swapped, token)
    if by_pairs:
        back_last = pass_on(back_next[-1], s_half)
        back_far = [swap(x, m) for x, m in zip([back[0], *back_next[:-1], back_last], far)]
        moment = moment_add(back_last, moment, both_last)
    basis, linv, left = basis_of(p_total, moment)
    q_mine = q_half(s_half, lax.ppermute(s_half, "dp", chip_pairs), linv, n_dp)
    q_other = lax.ppermute(q_mine, "dp", core_pairs)
    first_half = error_first(core, q_mine, left, moment)
    q_factor, error_out, token = error_second(core, q_mine, q_other, left, moment, first_half)
    if by_pairs:
        input_grad = unpack(token, pick_far, grad_near, back_far)
    else:
        input_grad = unpack_plain(count, order[0], returned, n_expert, capacity)
    return (input_grad[None], basis.T[None], q_factor.T[None], error_out[None, None])


def solution(mesh):
    placed = (
        P("dp", "expert", None),
        P("dp", "expert", None),
        P("dp", "expert"),
        P("dp", "expert", None, None),
        P("expert", None, None),
        P("dp", "expert", None, None),
        P("expert", None, None),
    )
    return jax.shard_map(
        functools.partial(shards, mesh.shape["expert"], mesh.shape["dp"]),
        mesh=mesh,
        in_specs=placed,
        out_specs=(
            P("dp", "expert", None),
            P("expert", None, None),
            P("expert", None, None),
            P("dp", "expert", None, None),
        ),
        check_vma=False,
    )
```

```python
import functools

import jax
import jax.numpy as jnp
from jax import lax
from jax.experimental import pallas as pl
from jax.experimental.pallas import tpu as pltpu
from jax.sharding import PartitionSpec as P

F32 = jnp.float32
BF16 = jnp.bfloat16
ROW_TILE = 16
COLS = 512
MIB = 1024 * 1024
FULL = 58


def whole_vmem():
    return pl.BlockSpec(memory_space=pltpu.VMEM)


def split3(x):
    hi = x.astype(BF16)
    rest = x - hi.astype(F32)
    mid = rest.astype(BF16)
    lo = (rest - mid.astype(F32)).astype(BF16)
    return hi, mid, lo


def stack3(x):
    return jnp.concatenate(split3(x), axis=0)


def fold3(x):
    n = x.shape[0] // 3
    return x[:n] + (x[n : 2 * n] + x[2 * n :])


def dot_nt(a, b):
    return lax.dot_general(a, b, (((1,), (1,)), ((), ())), preferred_element_type=F32)


def dot_nn(a, b):
    return jnp.dot(a, b, preferred_element_type=F32)


def full_dot(a, b):
    return jnp.dot(a, b, precision=lax.Precision.HIGHEST, preferred_element_type=F32)

def in_hbm():
    return pl.BlockSpec(memory_space=pltpu.HBM)


TOKEN = ((8, 128), F32)


def set_token(ref):
    ref[...] = jnp.zeros(ref.shape, ref.dtype)


def cost(flops, nbytes):
    return pl.CostEstimate(flops=flops, bytes_accessed=nbytes, transcendentals=0)


def call(kernel, name, scalars, operands, outs, scratch=(), limit=12, flops=10**9, nbytes=10**6, specs=None, out_specs=None):
    outs = [jax.ShapeDtypeStruct(shape, dtype) for shape, dtype in outs]
    return pl.pallas_call(
        kernel,
        grid_spec=pltpu.PrefetchScalarGridSpec(
            num_scalar_prefetch=len(scalars),
            grid=(),
            in_specs=specs or [whole_vmem()] * len(operands),
            out_specs=out_specs or [whole_vmem()] * len(outs),
            scratch_shapes=list(scratch),
        ),
        out_shape=outs,
        compiler_params=pltpu.CompilerParams(vmem_limit_bytes=limit * MIB),
        cost_estimate=cost(flops, nbytes),
        name=name,
    )(*scalars, *operands)


def start_of(counts_ref, expert, n):
    start = jnp.int32(0)
    for e in range(n):
        start = start + jnp.where(e < expert, counts_ref[0, e], 0)
    return start


def pack_first_kernel(n, mask, me_ref, core_ref, counts_hbm, rows_hbm, out_ref, counts_ref, rows_ref, sems):
    cap = out_ref.shape[0]
    total, window = rows_hbm.shape[0], rows_ref.shape[0]
    dest = me_ref[0] ^ mask
    base = jnp.clip(total - cap * (n - dest), 0, total - window)
    base = pl.multiple_of(base, ROW_TILE)
    copy_counts = pltpu.make_async_copy(counts_hbm, counts_ref, sems.at[0])
    copy_rows = pltpu.make_async_copy(rows_hbm.at[pl.ds(base, window), :], rows_ref, sems.at[1])
    copy_counts.start()
    copy_rows.start()
    copy_counts.wait()
    j = lax.broadcasted_iota(jnp.int32, (cap, window), 0)
    w = lax.broadcasted_iota(jnp.int32, (cap, window), 1)
    hit = (w == j + (start_of(counts_ref, dest, n) - base)) & (j < counts_ref[0, dest])
    pick = jnp.where(hit, 1.0, 0.0).astype(BF16)
    copy_rows.wait()
    out_ref[...] = dot_nn(pick, rows_ref[...]).astype(BF16)


def pack_first(me, core, counts, rows, n, cap, mask):
    total, width = rows.shape
    window = min(total, cap * (n + 1) - total)
    return call(
        functools.partial(pack_first_kernel, n, mask),
        "pack_first",
        (me, core),
        (counts, rows),
        [((cap, width), BF16)],
        [pltpu.SMEM(counts.shape, jnp.int32), pltpu.VMEM((window, width), BF16), pltpu.SemaphoreType.DMA((2,))],
        specs=[in_hbm()] * 2,
        limit=62,
        flops=10**6,
        nbytes=4 * 10**6,
    )[0]


def pack_kernel(n, cap, masks, me_ref, counts_hbm, rows_hbm, *rest):
    outs = rest[: len(masks)]
    counts_ref, rows_ref, held, sems, out_sems = rest[len(masks) :]
    total = rows_ref.shape[0]
    window = -(-(cap + ROW_TILE - 1) // ROW_TILE) * ROW_TILE
    copy_counts = pltpu.make_async_copy(counts_hbm, counts_ref, sems.at[0])
    copy_rows = pltpu.make_async_copy(rows_hbm, rows_ref, sems.at[1])
    copy_counts.start()
    copy_rows.start()
    copy_counts.wait()
    j = lax.broadcasted_iota(jnp.int32, (cap, window), 0)
    w = lax.broadcasted_iota(jnp.int32, (cap, window), 1)
    bases, picks = [], []
    for mask in masks:
        dest = me_ref[0] ^ mask
        start = start_of(counts_ref, dest, n)
        base = jnp.minimum((start // ROW_TILE) * ROW_TILE, total - window)
        bases.append(pl.multiple_of(base, ROW_TILE))
        hit = (w == j + (start - base)) & (j < counts_ref[0, dest])
        picks.append(jnp.where(hit, 1.0, 0.0).astype(BF16))
    copy_rows.wait()
    copies = []
    for k, (base, pick) in enumerate(zip(bases, picks)):
        held[k] = dot_nn(pick, rows_ref[pl.ds(base, window), :]).astype(BF16)
        copies.append(pltpu.make_async_copy(held.at[k], outs[k], out_sems.at[k]))
        copies[k].start()
    for copy in copies:
        copy.wait()


def pack(me, counts, rows, n, cap, masks):
    count, width = len(masks), rows.shape[1]
    return call(
        functools.partial(pack_kernel, n, cap, masks),
        "pack_rows",
        (me,),
        (counts, rows),
        [((cap, width), BF16)] * count,
        [
            pltpu.SMEM(counts.shape, jnp.int32),
            pltpu.VMEM(rows.shape, BF16),
            pltpu.VMEM((count, cap, width), BF16),
            pltpu.SemaphoreType.DMA((2,)),
            pltpu.SemaphoreType.DMA((count,)),
        ],
        specs=[in_hbm()] * 2,
        out_specs=[in_hbm()] * count,
        limit=FULL,
        flops=10**6,
        nbytes=10**4,
    )


def source_at(me_ref, slot, cap):
    if slot is None:
        return 0
    return pl.multiple_of((me_ref[0] ^ slot) * cap, ROW_TILE)


def place(chunks, slots, me_ref, hidden_ref, both_ref, at):
    cap, width = chunks[0].shape
    for k, slot in enumerate(slots):
        rows = pl.ds(at + k * cap, cap)
        both_ref[rows, :width] = chunks[k][...]
        both_ref[rows, width:] = hidden_ref[pl.ds(source_at(me_ref, slot, cap), cap), :]


def p_term(q, rows, hidden):
    return fold3(dot_nn(stack3(dot_nt(q, rows)), hidden))


def early_kernel(slots, me_ref, q_ref, hidden_ref, error_ref, weight_ref, *rest):
    chunks = rest[: len(slots)]
    p_ref, both_ref, moment_ref, *slot_refs = rest[len(slots) :]
    cap = chunks[0].shape[0]
    width = error_ref.shape[1]
    place(chunks, slots, me_ref, hidden_ref, both_ref, 0)
    q = q_ref[...]
    p_ref[...] = dot_nt(q, error_ref[...]) + p_term(q, both_ref[:, :width], both_ref[:, width:])
    hidden_t = both_ref[:, width:].T
    for j in range(0, width, COLS):
        block = dot_nn(hidden_t, both_ref[:, j : j + COLS])
        moment_ref[:, j : j + COLS] = error_ref[:, j : j + COLS].astype(F32) + block
    res = dot_nt(both_ref[:, :width], weight_ref[...]).astype(BF16)
    for k, ref in enumerate(slot_refs):
        ref[...] = res[k * cap : (k + 1) * cap]


def early_part(me, q, hidden, error, weight, chunks, slots):
    cap, width = chunks[0].shape
    ff = hidden.shape[1]
    rows = cap * len(slots)
    return call(
        functools.partial(early_kernel, slots),
        "early_rows",
        (me,),
        (q, hidden, error, weight, *chunks),
        [((q.shape[0], ff), F32), ((rows, width + ff), BF16), ((ff, width), F32)]
        + [((cap, ff), BF16)] * len(slots),
        flops=2 * 10**9,
        nbytes=10**7,
    )


def late_kernel(slots, me_ref, weight_ref, q_ref, hidden_ref, base_ref, *rest):
    chunks, (p_ref, both_ref) = rest[: len(slots)], rest[len(slots) :]
    width = chunks[0].shape[1]
    place(chunks, slots, me_ref, hidden_ref, both_ref, 0)
    p_ref[...] = base_ref[...] + p_term(q_ref[...], both_ref[:, :width], both_ref[:, width:])


def late_part(me, weight, q, hidden, base, chunks, slots):
    cap, width = chunks[0].shape
    ff = hidden.shape[1]
    return call(
        functools.partial(late_kernel, slots),
        "late_rows",
        (me,),
        (weight, q, hidden, base, *chunks),
        [((q.shape[0], ff), F32), ((cap * len(slots), width + ff), BF16)],
        flops=10**6,
        nbytes=10**4,
    )


def slot_kernel(at, count, both_ref, weight_ref, *rest):
    outs = rest[len(rest) - count :]
    cap, width = outs[0].shape[0], weight_ref.shape[1]
    res = dot_nt(both_ref[at : at + cap * count, :width], weight_ref[...]).astype(BF16)
    for k, out in enumerate(outs):
        out[...] = res[k * cap : (k + 1) * cap]


def slot_grads(both, weight, before, at, cap, count, flops):
    return call(
        functools.partial(slot_kernel, at, count),
        "slot_grads",
        (),
        (both, weight, *before),
        [((cap, weight.shape[0]), BF16)] * count,
        flops=flops,
        nbytes=10**4,
    )


def s_columns(part, p3, ys, error_ref, groups, out_ref):
    half = out_ref.shape[1]
    for j in range(0, half, COLS):
        cols = pl.ds(pl.multiple_of(part * half + j, COLS), COLS)
        res = dot_nn(p3, error_ref[:, cols])
        for y, group in zip(ys, groups):
            res = res + dot_nn(y, group[:, cols])
        out_ref[:, j : j + COLS] = fold3(res)


def s_send_kernel(count, core_ref, before_ref, pa_ref, pb_ref, error_ref, *rest):
    groups = rest[:count]
    p_out, send_ref, p3_ref, *y_refs = rest[count:]
    total = pa_ref[...] + pb_ref[...]
    p_out[...] = total
    p3_ref[...] = stack3(total)
    width = error_ref.shape[1]
    for y_ref, group in zip(y_refs, groups):
        y_ref[...] = stack3(fold3(dot_nt(p3_ref[...], group[:, width:])))
    s_columns(1 - core_ref[0], p3_ref[...], [y[...] for y in y_refs], error_ref, groups, send_ref)


def s_send(core, before, pa, pb, error, groups):
    rank, ff = pa.shape
    width = error.shape[1]
    return call(
        functools.partial(s_send_kernel, len(groups)),
        "s_send",
        (core,),
        (before, pa, pb, error, *groups),
        [((rank, ff), F32), ((rank, width // 2), F32), ((3 * rank, ff), BF16)]
        + [((3 * rank, group.shape[0]), BF16) for group in groups],
        nbytes=7 * 10**6,
    )


def s_keep_kernel(count, core_ref, p3_ref, error_ref, *rest):
    ys, groups, (keep_ref, token_ref) = rest[:count], rest[count : 2 * count], rest[2 * count :]
    set_token(token_ref)
    s_columns(core_ref[0], p3_ref[...], [y[...] for y in ys], error_ref, groups, keep_ref)


def s_keep(core, p3, ys, error, groups):
    rank = p3.shape[0] // 3
    return call(
        functools.partial(s_keep_kernel, len(groups)),
        "s_keep",
        (core,),
        (p3, error, *ys, *groups),
        [((rank, error.shape[1] // 2), F32), TOKEN],
        nbytes=7 * 10**6,
    )


def basis_kernel(p_ref, before_ref, basis_ref, linv_ref, left_ref):
    p = p_ref[...]
    rank = p.shape[0]
    p3 = stack3(p)
    gram_rows = fold3(dot_nt(p3, p3))
    gram = gram_rows[:, :rank] + (gram_rows[:, rank : 2 * rank] + gram_rows[:, 2 * rank :])
    row = lax.broadcasted_iota(jnp.int32, (rank, rank), 0)
    col = lax.broadcasted_iota(jnp.int32, (rank, rank), 1)
    eye = jnp.where(row == col, 1.0, 0.0)
    aug = jnp.concatenate([gram, eye], axis=1)
    sub, group = 8, 4
    shape = (sub, 2 * rank)
    blocks = [aug[b * sub : (b + 1) * sub] for b in range(rank // sub)]
    sub_id = lax.broadcasted_iota(jnp.int32, shape, 0)
    for k in range(0, rank, group):
        kb, kr = divmod(k, sub)
        spread = {
            (b, i): jnp.broadcast_to(blocks[b][:, k + i : k + i + 1], shape)
            for b in range(kb, rank // sub)
            for i in range(group)
        }
        low, scale, pivots = {}, [], []
        for i in range(group):
            for j in range(i + 1):
                left = jnp.broadcast_to(spread[kb, j][kr + i : kr + i + 1], shape)
                for m in range(j):
                    left = left - low[i, m] * low[j, m]
                low[i, j] = left * scale[j] if j < i else left
            scale.append(lax.rsqrt(low[i, i]))
            pivot = jnp.broadcast_to(blocks[kb][kr + i : kr + i + 1], shape)
            for m in range(i):
                pivot = pivot - low[i, m] * pivots[m]
            pivots.append(pivot * scale[i])
        for b in range(kb, rank // sub):
            updated, factors = blocks[b], []
            for i in range(group):
                factor = spread[b, i]
                for m in range(i):
                    factor = factor - factors[m] * low[i, m]
                factors.append(factor * scale[i])
                updated = updated - factors[i] * pivots[i]
            if b == kb:
                updated = jnp.where(sub_id >= kr + group, updated, blocks[b])
                for i in range(group):
                    updated = jnp.where(sub_id == kr + i, pivots[i], updated)
            blocks[b] = updated
    linv = jnp.concatenate(blocks, axis=0)[:, rank:]
    linv_ref[...] = linv
    basis = full_dot(linv, p)
    basis_ref[...] = basis
    hi, mid, lo = split3(basis)
    left_ref[...] = jnp.concatenate([hi, hi, mid, mid, hi, lo], axis=0).T


def basis_of(p, before):
    rank, ff = p.shape
    return call(
        basis_kernel,
        "basis",
        (),
        (p, before),
        [((rank, ff), F32), ((rank, rank), F32), ((ff, 6 * rank), BF16)],
        flops=10**10,
    )


def moment_kernel(before_ref, moment_ref, both_ref, out_ref):
    width = out_ref.shape[1]
    hidden_t = both_ref[:, width:].T
    for j in range(0, width, COLS):
        cols = slice(j, j + COLS)
        out_ref[:, cols] = moment_ref[:, cols] + dot_nn(hidden_t, both_ref[:, cols])


def moment_add(before, moment, both):
    return call(
        moment_kernel,
        "moment_add",
        (),
        (before, moment, both),
        [(moment.shape, F32)],
        flops=10**10,
    )[0]


def q_kernel(replicas, mine_ref, far_ref, linv_ref, out_ref):
    out_ref[...] = full_dot(linv_ref[...], mine_ref[...] + far_ref[...]) * (1.0 / replicas)


def q_half(mine, far, linv, replicas):
    return call(functools.partial(q_kernel, replicas), "q_half", (), (mine, far, linv), [(mine.shape, F32)])[0]


def error_block(part, k, block, q_ref, left_ref, moment_ref, right):
    rank, half = q_ref.shape
    here = pl.ds(k * block, block)
    cols = pl.ds(pl.multiple_of(part * half + k * block, block), block)
    hi, mid, lo = split3(-q_ref[:, here])
    for i, piece in enumerate((hi, mid, hi, mid, lo, hi)):
        right[i * rank : (i + 1) * rank, here] = piece
    return (moment_ref[:, cols] + dot_nn(left_ref[...], right[:, here])).astype(BF16)


def error_first_kernel(block, core_ref, q_ref, left_ref, moment_ref, out_ref, right):
    for k in range(q_ref.shape[1] // block):
        here = pl.ds(k * block, block)
        out_ref[:, here] = error_block(core_ref[0], k, block, q_ref, left_ref, moment_ref, right)


def error_first(core, q, left, moment):
    half = q.shape[1]
    return call(
        functools.partial(error_first_kernel, 256),
        "new_error_first",
        (core,),
        (q, left, moment),
        [((moment.shape[0], half), BF16)],
        [pltpu.VMEM((left.shape[1], half), BF16)],
        flops=10**10,
    )[0]


def last_kernel(block, parts, core_ref, mine_ref, other_ref, left_ref, moment_ref, first_ref, *rest):
    count = len(rest) - (10 if parts else 5)
    chunks = rest[2 : 2 + count] if parts else ()
    near_ref, pick_ref = rest[:2] if parts else (None, None)
    outs = rest[2 + count :] if parts else rest
    q_hbm, out_hbm = outs[:2]
    right, held, sems = outs[-3:]
    half = mine_ref.shape[1]
    part = 1 - core_ref[0]
    at_mine = pl.ds(pl.multiple_of(core_ref[0] * half, half), half)
    at_other = pl.ds(pl.multiple_of(part * half, half), half)
    copies = [
        pltpu.make_async_copy(first_ref, out_hbm.at[:, at_mine], sems.at[0]),
        pltpu.make_async_copy(mine_ref, q_hbm.at[:, at_mine], sems.at[1]),
        pltpu.make_async_copy(other_ref, q_hbm.at[:, at_other], sems.at[2]),
    ]
    for copy in copies:
        copy.start()
    steps = half // block
    for k in range(steps):
        here = pl.ds(k * block, block)
        cols = pl.ds(pl.multiple_of(part * half + k * block, block), block)
        held[:, here] = error_block(part, k, block, other_ref, left_ref, moment_ref, right)
        copies.append(pltpu.make_async_copy(held.at[:, here], out_hbm.at[:, cols], sems.at[3 + k]))
        copies[-1].start()
    if parts:
        grad_hbm, cat, grad_ref = outs[2:5]
        cap = chunks[0].shape[0]
        for k in range(count):
            cat[k * cap : (k + 1) * cap, :] = chunks[k][...]
        rows = grad_ref.shape[0] // parts
        for k in range(parts):
            at = pl.ds(k * rows, rows)
            grad_ref[at, :] = near_ref[at, :] + dot_nn(pick_ref[at, :], cat[...]).astype(BF16)
            copies.append(pltpu.make_async_copy(grad_ref.at[at, :], grad_hbm.at[at, :], sems.at[3 + steps + k]))
            copies[-1].start()
    for copy in copies:
        copy.wait()


def last_part(core, mine, other, left, moment, first, near=None, pick=None, chunks=()):
    ff, width = moment.shape
    rank, half = mine.shape
    block = 256
    parts = 2 if chunks else 0
    operands = [mine, other, left, moment, first]
    outs = [((rank, width), F32), ((ff, width), BF16)]
    scratch = []
    if chunks:
        operands += [near, pick, *chunks]
        outs.append((near.shape, BF16))
        scratch = [pltpu.VMEM((pick.shape[1], ff), BF16), pltpu.VMEM(near.shape, BF16)]
    scratch += [
        pltpu.VMEM((left.shape[1], half), BF16),
        pltpu.VMEM((ff, half), BF16),
        pltpu.SemaphoreType.DMA((3 + half // block + parts,)),
    ]
    return call(
        functools.partial(last_kernel, block, parts),
        "new_error_last",
        (core,),
        operands,
        outs,
        scratch,
        out_specs=[in_hbm()] * len(outs),
        flops=10**10,
    )


def pick_kernel(n, cap, masks, me_ref, counts_ref, order_ref, out_ref, held):
    order = order_ref[...]
    j = lax.broadcasted_iota(jnp.int32, (cap, order.shape[1]), 0)
    for k, mask in enumerate(masks):
        expert = me_ref[0] ^ mask
        start = jnp.int32(0)
        for e in range(n):
            start = start + jnp.where(e < expert, counts_ref[e], 0)
        hit = (order == j + start) & (j < counts_ref[expert])
        held[k * cap : (k + 1) * cap, :] = jnp.where(hit, 1.0, 0.0)
    out_ref[...] = held[...].T.astype(BF16)


def pick_of(me, counts, order, n, cap, masks):
    tokens = order.shape[1]
    slots = len(masks) * cap
    return call(
        functools.partial(pick_kernel, n, cap, masks),
        "pick_rows",
        (me, counts),
        (order,),
        [((tokens, slots), BF16)],
        [pltpu.VMEM((slots, tokens), F32)],
        flops=10**6,
        nbytes=10**4,
    )[0]


def unpack_first_kernel(count, before_ref, pick_ref, *rest):
    chunks, (out_ref, token_ref, cat) = rest[:count], rest[count:]
    cap = chunks[0].shape[0]
    for k in range(count):
        cat[k * cap : (k + 1) * cap, :] = chunks[k][...]
    out_ref[...] = dot_nn(pick_ref[...], cat[...]).astype(BF16)
    set_token(token_ref)


def unpack_first(before, pick, chunks):
    cap, ff = chunks[0].shape
    return call(
        functools.partial(unpack_first_kernel, len(chunks)),
        "unpack_first",
        (),
        (before, pick, *chunks),
        [((pick.shape[0], ff), BF16), TOKEN],
        [pltpu.VMEM((len(chunks) * cap, ff), BF16)],
        flops=10**10,
    )


def pack_plain(route_count, local_rows, experts, capacity):
    total_rows, width = local_rows.shape
    route_starts = jnp.cumsum(route_count) - route_count
    slot_ids = jnp.arange(capacity, dtype=jnp.int32)
    pick_index = jnp.minimum(route_starts[:, None] + slot_ids[None, :], total_rows - 1)
    slot_valid = slot_ids[None, :] < route_count[:, None]
    outgoing = local_rows[pick_index.reshape(-1)].reshape(experts, capacity, width)
    return jnp.where(slot_valid[:, :, None], outgoing, jnp.zeros((), BF16))


def unpack_plain(route_count, order_local, returned, experts, capacity):
    route_ends = jnp.cumsum(route_count)
    route_starts = route_ends - route_count
    expert_of = jnp.sum((route_ends[None, :] <= order_local[:, None]).astype(jnp.int32), axis=1)
    row_base = jnp.arange(experts, dtype=jnp.int32) * capacity - route_starts
    return returned[row_base[expert_of] + order_local]


def gap_kernel(*refs):
    set_token(refs[-1])


def gap(*before):
    return call(gap_kernel, "gap", (), before, [TOKEN], limit=4, flops=10**10)[0]


def add_kernel(a_ref, b_ref, *rest):
    rest[-1][...] = a_ref[...] + b_ref[...]


def add(a, b, *before):
    return call(add_kernel, "add", (), (a, b, *before), [(a.shape, F32)], limit=4, flops=10**6)[0]


def pass_kernel(x_ref, before_ref, out_ref):
    out_ref[...] = x_ref[...]


def pass_on(x, before):
    return call(pass_kernel, "pass_on", (), (x, before), [(x.shape, x.dtype)], limit=4, flops=10**6)[0]


def shards(n_expert, n_dp, grad_rows, counts, order, hidden, down_weight, error_in, q_init):
    rows = grad_rows[0]
    count = counts[0, 0]
    saved = hidden[0, 0]
    weight = down_weight[0]
    error = error_in[0, 0]
    q = q_init[0].T
    ff = saved.shape[1]
    capacity = saved.shape[0] // n_expert
    me = lax.axis_index("expert").astype(jnp.int32)[None]
    core = (lax.axis_index("dp").astype(jnp.int32) & 1)[None]
    core_pairs = [(d, d ^ 1) for d in range(n_dp)]
    chip_pairs = [(d, d ^ 2) for d in range(n_dp)]
    by_pairs = n_expert == 8 and capacity % ROW_TILE == 0 and rows.shape[0] % ROW_TILE == 0

    if by_pairs:
        far = tuple(reversed(range(n_expert // 2, n_expert)))
        near = tuple(reversed(range(0, n_expert // 2)))
        first, last = far[:1] + near, far[1:]

        def swap(x, mask):
            return lax.ppermute(x, "expert", [(e, e ^ mask) for e in range(n_expert)])

        others = far[1:] + near
        packed = {far[0]: pack_first(me, core, counts[0], rows, n_expert, capacity, far[0])}
        packed.update(zip(others, pack(me, counts[0], rows, n_expert, capacity, others)))
        arrived = {m: swap(packed[m], m) if m else packed[m] for m in far + near}
        pick_near = pick_of(me, count, order, n_expert, capacity, near)
        pick_far = pick_of(me, count, order, n_expert, capacity, far)
        p_first, both_first, moment, *back = early_part(
            me, q, saved, error, weight, [arrived[m] for m in first], first
        )
        back_near = [swap(x, m) if m else x for x, m in zip(back[1:], near)]
        p_mine, both_last = late_part(me, weight, q, saved, p_first, [arrived[m] for m in last], last)
        back_soon = pass_on(back[0], p_mine)
        before = [gap(p_mine, pick_near, pick_far, *back_near)]
        groups = [both_first, both_last]
    else:
        outgoing = pack_plain(count, rows, n_expert, capacity)
        arrived = lax.all_to_all(outgoing, "expert", split_axis=0, concat_axis=0, tiled=True)
        arrived = arrived.reshape(n_expert * capacity, rows.shape[1])
        p_mine, both_first, moment, back = early_part(me, q, saved, error, weight, [arrived], (None,))
        before, groups = [], [both_first]
        back = back.reshape(n_expert, capacity, ff)
        returned = lax.all_to_all(back, "expert", split_axis=0, concat_axis=0, tiled=True)
        returned = returned.reshape(n_expert * capacity, ff)
    p_chip = add(p_mine, lax.ppermute(p_mine, "dp", core_pairs), *before)
    p_far = lax.ppermute(p_chip, "dp", chip_pairs)
    before = p_chip
    if by_pairs:
        back_next = slot_grads(both_last, weight, (p_chip,), 0, capacity, len(last), 10**6)
        moment = moment_add(back_next[0], moment, both_last)
        before = back_next[0]
    p_total, s_sent, p3, *ys = s_send(core, before, p_chip, p_far, error, groups)
    s_swapped = lax.ppermute(s_sent, "dp", core_pairs)
    s_kept, token = s_keep(core, p3, ys, error, groups)
    if by_pairs:
        grad_near, token = unpack_first(token, pick_near, back_near)
    s_half = add(s_kept, s_swapped, token)
    if by_pairs:
        back_last = pass_on(back_next[-1], s_half)
        back_far = [swap(x, m) for x, m in zip([back_soon, *back_next[:-1], back_last], far)]
    basis, linv, left = basis_of(p_total, back_last if by_pairs else p_total)
    q_mine = q_half(s_half, lax.ppermute(s_half, "dp", chip_pairs), linv, n_dp)
    q_other = lax.ppermute(q_mine, "dp", core_pairs)
    first_half = error_first(core, q_mine, left, moment)
    if by_pairs:
        q_factor, error_out, input_grad = last_part(
            core, q_mine, q_other, left, moment, first_half, grad_near, pick_far, back_far
        )
    else:
        q_factor, error_out = last_part(core, q_mine, q_other, left, moment, first_half)
        input_grad = unpack_plain(count, order[0], returned, n_expert, capacity)
    return (input_grad[None], basis.T[None], q_factor.T[None], error_out[None, None])


def solution(mesh):
    placed = (
        P("dp", "expert", None),
        P("dp", "expert", None),
        P("dp", "expert"),
        P("dp", "expert", None, None),
        P("expert", None, None),
        P("dp", "expert", None, None),
        P("expert", None, None),
    )
    return jax.shard_map(
        functools.partial(shards, mesh.shape["expert"], mesh.shape["dp"]),
        mesh=mesh,
        in_specs=placed,
        out_specs=(
            P("dp", "expert", None),
            P("expert", None, None),
            P("expert", None, None),
            P("dp", "expert", None, None),
        ),
        check_vma=False,
    )
```

```python
import functools

import jax
import jax.numpy as jnp
from jax import lax
from jax.experimental import pallas as pl
from jax.experimental.pallas import tpu as pltpu
from jax.sharding import PartitionSpec as P

F32 = jnp.float32
BF16 = jnp.bfloat16
ROW_TILE = 16
COLS = 512
MIB = 1024 * 1024
FULL = 58


def whole_vmem():
    return pl.BlockSpec(memory_space=pltpu.VMEM)


def split3(x):
    hi = x.astype(BF16)
    rest = x - hi.astype(F32)
    mid = rest.astype(BF16)
    lo = (rest - mid.astype(F32)).astype(BF16)
    return hi, mid, lo


def stack3(x):
    return jnp.concatenate(split3(x), axis=0)


def fold3(x):
    n = x.shape[0] // 3
    return x[:n] + (x[n : 2 * n] + x[2 * n :])


def dot_nt(a, b):
    return lax.dot_general(a, b, (((1,), (1,)), ((), ())), preferred_element_type=F32)


def dot_nn(a, b):
    return jnp.dot(a, b, preferred_element_type=F32)


def full_dot(a, b):
    return jnp.dot(a, b, precision=lax.Precision.HIGHEST, preferred_element_type=F32)

def in_hbm():
    return pl.BlockSpec(memory_space=pltpu.HBM)


TOKEN = ((8, 128), F32)


def set_token(ref):
    ref[...] = jnp.zeros(ref.shape, ref.dtype)


def cost(flops, nbytes):
    return pl.CostEstimate(flops=flops, bytes_accessed=nbytes, transcendentals=0)


def call(kernel, name, scalars, operands, outs, scratch=(), limit=12, flops=10**9, nbytes=10**6, specs=None, out_specs=None):
    outs = [jax.ShapeDtypeStruct(shape, dtype) for shape, dtype in outs]
    return pl.pallas_call(
        kernel,
        grid_spec=pltpu.PrefetchScalarGridSpec(
            num_scalar_prefetch=len(scalars),
            grid=(),
            in_specs=specs or [whole_vmem()] * len(operands),
            out_specs=out_specs or [whole_vmem()] * len(outs),
            scratch_shapes=list(scratch),
        ),
        out_shape=outs,
        compiler_params=pltpu.CompilerParams(vmem_limit_bytes=limit * MIB),
        cost_estimate=cost(flops, nbytes),
        name=name,
    )(*scalars, *operands)


def start_of(counts_ref, expert, n):
    start = jnp.int32(0)
    for e in range(n):
        start = start + jnp.where(e < expert, counts_ref[0, e], 0)
    return start


def pack_first_kernel(n, mask, me_ref, core_ref, counts_hbm, rows_hbm, out_ref, counts_ref, rows_ref, sems):
    cap = out_ref.shape[0]
    total, window = rows_hbm.shape[0], rows_ref.shape[0]
    dest = me_ref[0] ^ mask
    base = jnp.clip(total - cap * (n - dest), 0, total - window)
    base = pl.multiple_of(base, ROW_TILE)
    copy_counts = pltpu.make_async_copy(counts_hbm, counts_ref, sems.at[0])
    copy_rows = pltpu.make_async_copy(rows_hbm.at[pl.ds(base, window), :], rows_ref, sems.at[1])
    copy_counts.start()
    copy_rows.start()
    copy_counts.wait()
    j = lax.broadcasted_iota(jnp.int32, (cap, window), 0)
    w = lax.broadcasted_iota(jnp.int32, (cap, window), 1)
    hit = (w == j + (start_of(counts_ref, dest, n) - base)) & (j < counts_ref[0, dest])
    pick = jnp.where(hit, 1.0, 0.0).astype(BF16)
    copy_rows.wait()
    out_ref[...] = dot_nn(pick, rows_ref[...]).astype(BF16)


def pack_first(me, core, counts, rows, n, cap, mask):
    total, width = rows.shape
    window = min(total, cap * (n + 1) - total)
    return call(
        functools.partial(pack_first_kernel, n, mask),
        "pack_first",
        (me, core),
        (counts, rows),
        [((cap, width), BF16)],
        [pltpu.SMEM(counts.shape, jnp.int32), pltpu.VMEM((window, width), BF16), pltpu.SemaphoreType.DMA((2,))],
        specs=[in_hbm()] * 2,
        limit=62,
        flops=10**6,
        nbytes=4 * 10**6,
    )[0]


def pack_kernel(n, cap, masks, me_ref, counts_hbm, rows_hbm, *rest):
    outs = rest[: len(masks)]
    counts_ref, rows_ref, held, sems, out_sems = rest[len(masks) :]
    total = rows_ref.shape[0]
    window = -(-(cap + ROW_TILE - 1) // ROW_TILE) * ROW_TILE
    copy_counts = pltpu.make_async_copy(counts_hbm, counts_ref, sems.at[0])
    copy_rows = pltpu.make_async_copy(rows_hbm, rows_ref, sems.at[1])
    copy_counts.start()
    copy_rows.start()
    copy_counts.wait()
    j = lax.broadcasted_iota(jnp.int32, (cap, window), 0)
    w = lax.broadcasted_iota(jnp.int32, (cap, window), 1)
    bases, picks = [], []
    for mask in masks:
        dest = me_ref[0] ^ mask
        start = start_of(counts_ref, dest, n)
        base = jnp.minimum((start // ROW_TILE) * ROW_TILE, total - window)
        bases.append(pl.multiple_of(base, ROW_TILE))
        hit = (w == j + (start - base)) & (j < counts_ref[0, dest])
        picks.append(jnp.where(hit, 1.0, 0.0).astype(BF16))
    copy_rows.wait()
    copies = []
    for k, (base, pick) in enumerate(zip(bases, picks)):
        held[k] = dot_nn(pick, rows_ref[pl.ds(base, window), :]).astype(BF16)
        copies.append(pltpu.make_async_copy(held.at[k], outs[k], out_sems.at[k]))
        copies[k].start()
    for copy in copies:
        copy.wait()


def pack(me, counts, rows, n, cap, masks):
    count, width = len(masks), rows.shape[1]
    return call(
        functools.partial(pack_kernel, n, cap, masks),
        "pack_rows",
        (me,),
        (counts, rows),
        [((cap, width), BF16)] * count,
        [
            pltpu.SMEM(counts.shape, jnp.int32),
            pltpu.VMEM(rows.shape, BF16),
            pltpu.VMEM((count, cap, width), BF16),
            pltpu.SemaphoreType.DMA((2,)),
            pltpu.SemaphoreType.DMA((count,)),
        ],
        specs=[in_hbm()] * 2,
        out_specs=[in_hbm()] * count,
        limit=FULL,
        flops=10**6,
        nbytes=10**4,
    )


def source_at(me_ref, slot, cap):
    if slot is None:
        return 0
    return pl.multiple_of((me_ref[0] ^ slot) * cap, ROW_TILE)


def place(chunks, slots, me_ref, hidden_ref, both_ref, at):
    cap, width = chunks[0].shape
    for k, slot in enumerate(slots):
        rows = pl.ds(at + k * cap, cap)
        both_ref[rows, :width] = chunks[k][...]
        both_ref[rows, width:] = hidden_ref[pl.ds(source_at(me_ref, slot, cap), cap), :]


def p_term(q, rows, hidden):
    return fold3(dot_nn(stack3(dot_nt(q, rows)), hidden))


def early_kernel(slots, me_ref, q_ref, hidden_ref, error_ref, weight_ref, *rest):
    chunks = rest[: len(slots)]
    p_ref, both_ref, moment_ref, *slot_refs = rest[len(slots) :]
    cap = chunks[0].shape[0]
    width = error_ref.shape[1]
    place(chunks, slots, me_ref, hidden_ref, both_ref, 0)
    q = q_ref[...]
    p_ref[...] = dot_nt(q, error_ref[...]) + p_term(q, both_ref[:, :width], both_ref[:, width:])
    hidden_t = both_ref[:, width:].T
    for j in range(0, width, COLS):
        block = dot_nn(hidden_t, both_ref[:, j : j + COLS])
        moment_ref[:, j : j + COLS] = error_ref[:, j : j + COLS].astype(F32) + block
    res = dot_nt(both_ref[:, :width], weight_ref[...]).astype(BF16)
    for k, ref in enumerate(slot_refs):
        ref[...] = res[k * cap : (k + 1) * cap]


def early_part(me, q, hidden, error, weight, chunks, slots):
    cap, width = chunks[0].shape
    ff = hidden.shape[1]
    rows = cap * len(slots)
    return call(
        functools.partial(early_kernel, slots),
        "early_rows",
        (me,),
        (q, hidden, error, weight, *chunks),
        [((q.shape[0], ff), F32), ((rows, width + ff), BF16), ((ff, width), F32)]
        + [((cap, ff), BF16)] * len(slots),
        flops=2 * 10**9,
        nbytes=10**7,
    )


def late_kernel(slots, me_ref, weight_ref, q_ref, hidden_ref, base_ref, *rest):
    chunks, (p_ref, both_ref) = rest[: len(slots)], rest[len(slots) :]
    width = chunks[0].shape[1]
    place(chunks, slots, me_ref, hidden_ref, both_ref, 0)
    p_ref[...] = base_ref[...] + p_term(q_ref[...], both_ref[:, :width], both_ref[:, width:])


def late_part(me, weight, q, hidden, base, chunks, slots):
    cap, width = chunks[0].shape
    ff = hidden.shape[1]
    return call(
        functools.partial(late_kernel, slots),
        "late_rows",
        (me,),
        (weight, q, hidden, base, *chunks),
        [((q.shape[0], ff), F32), ((cap * len(slots), width + ff), BF16)],
        flops=10**6,
        nbytes=10**4,
    )


def slot_kernel(at, count, both_ref, weight_ref, *rest):
    outs = rest[len(rest) - count :]
    cap, width = outs[0].shape[0], weight_ref.shape[1]
    res = dot_nt(both_ref[at : at + cap * count, :width], weight_ref[...]).astype(BF16)
    for k, out in enumerate(outs):
        out[...] = res[k * cap : (k + 1) * cap]


def slot_grads(both, weight, before, at, cap, count, flops):
    return call(
        functools.partial(slot_kernel, at, count),
        "slot_grads",
        (),
        (both, weight, *before),
        [((cap, weight.shape[0]), BF16)] * count,
        flops=flops,
        nbytes=10**4,
    )


def s_columns(part, p3, ys, error_ref, groups, out_ref):
    half = out_ref.shape[1]
    for j in range(0, half, COLS):
        cols = pl.ds(pl.multiple_of(part * half + j, COLS), COLS)
        res = dot_nn(p3, error_ref[:, cols])
        for y, group in zip(ys, groups):
            res = res + dot_nn(y, group[:, cols])
        out_ref[:, j : j + COLS] = fold3(res)


def s_send_kernel(count, core_ref, before_ref, pa_ref, pb_ref, error_ref, *rest):
    groups = rest[:count]
    p_out, send_ref, p3_ref, *y_refs = rest[count:]
    total = pa_ref[...] + pb_ref[...]
    p_out[...] = total
    p3_ref[...] = stack3(total)
    width = error_ref.shape[1]
    for y_ref, group in zip(y_refs, groups):
        y_ref[...] = stack3(fold3(dot_nt(p3_ref[...], group[:, width:])))
    s_columns(1 - core_ref[0], p3_ref[...], [y[...] for y in y_refs], error_ref, groups, send_ref)


def s_send(core, before, pa, pb, error, groups):
    rank, ff = pa.shape
    width = error.shape[1]
    return call(
        functools.partial(s_send_kernel, len(groups)),
        "s_send",
        (core,),
        (before, pa, pb, error, *groups),
        [((rank, ff), F32), ((rank, width // 2), F32), ((3 * rank, ff), BF16)]
        + [((3 * rank, group.shape[0]), BF16) for group in groups],
        nbytes=7 * 10**6,
    )


def s_keep_kernel(count, core_ref, p3_ref, error_ref, *rest):
    ys, groups, (keep_ref, token_ref) = rest[:count], rest[count : 2 * count], rest[2 * count :]
    set_token(token_ref)
    s_columns(core_ref[0], p3_ref[...], [y[...] for y in ys], error_ref, groups, keep_ref)


def s_keep(core, p3, ys, error, groups):
    rank = p3.shape[0] // 3
    return call(
        functools.partial(s_keep_kernel, len(groups)),
        "s_keep",
        (core,),
        (p3, error, *ys, *groups),
        [((rank, error.shape[1] // 2), F32), TOKEN],
        nbytes=7 * 10**6,
    )


def basis_kernel(p_ref, before_ref, basis_ref, linv_ref, left_ref):
    p = p_ref[...]
    rank = p.shape[0]
    p3 = stack3(p)
    gram_rows = fold3(dot_nt(p3, p3))
    gram = gram_rows[:, :rank] + (gram_rows[:, rank : 2 * rank] + gram_rows[:, 2 * rank :])
    row = lax.broadcasted_iota(jnp.int32, (rank, rank), 0)
    col = lax.broadcasted_iota(jnp.int32, (rank, rank), 1)
    eye = jnp.where(row == col, 1.0, 0.0)
    aug = jnp.concatenate([gram, eye], axis=1)
    sub, group = 8, 4
    shape = (sub, 2 * rank)
    blocks = [aug[b * sub : (b + 1) * sub] for b in range(rank // sub)]
    sub_id = lax.broadcasted_iota(jnp.int32, shape, 0)
    for k in range(0, rank, group):
        kb, kr = divmod(k, sub)
        spread = {
            (b, i): jnp.broadcast_to(blocks[b][:, k + i : k + i + 1], shape)
            for b in range(kb, rank // sub)
            for i in range(group)
        }
        low, scale, pivots = {}, [], []
        for i in range(group):
            for j in range(i + 1):
                left = jnp.broadcast_to(spread[kb, j][kr + i : kr + i + 1], shape)
                for m in range(j):
                    left = left - low[i, m] * low[j, m]
                low[i, j] = left * scale[j] if j < i else left
            scale.append(lax.rsqrt(low[i, i]))
            pivot = jnp.broadcast_to(blocks[kb][kr + i : kr + i + 1], shape)
            for m in range(i):
                pivot = pivot - low[i, m] * pivots[m]
            pivots.append(pivot * scale[i])
        for b in range(kb, rank // sub):
            updated, factors = blocks[b], []
            for i in range(group):
                factor = spread[b, i]
                for m in range(i):
                    factor = factor - factors[m] * low[i, m]
                factors.append(factor * scale[i])
                updated = updated - factors[i] * pivots[i]
            if b == kb:
                updated = jnp.where(sub_id >= kr + group, updated, blocks[b])
                for i in range(group):
                    updated = jnp.where(sub_id == kr + i, pivots[i], updated)
            blocks[b] = updated
    linv = jnp.concatenate(blocks, axis=0)[:, rank:]
    linv_ref[...] = linv
    basis = full_dot(linv, p)
    basis_ref[...] = basis
    hi, mid, lo = split3(basis)
    left_ref[...] = jnp.concatenate([hi, hi, mid, mid, hi, lo], axis=0).T


def basis_of(p, before):
    rank, ff = p.shape
    return call(
        basis_kernel,
        "basis",
        (),
        (p, before),
        [((rank, ff), F32), ((rank, rank), F32), ((ff, 6 * rank), BF16)],
        flops=10**10,
    )


def moment_kernel(before_ref, moment_ref, both_ref, out_ref):
    width = out_ref.shape[1]
    hidden_t = both_ref[:, width:].T
    for j in range(0, width, COLS):
        cols = slice(j, j + COLS)
        out_ref[:, cols] = moment_ref[:, cols] + dot_nn(hidden_t, both_ref[:, cols])


def moment_add(before, moment, both):
    return call(
        moment_kernel,
        "moment_add",
        (),
        (before, moment, both),
        [(moment.shape, F32)],
        flops=10**10,
    )[0]


def q_kernel(replicas, mine_ref, far_ref, linv_ref, out_ref):
    out_ref[...] = full_dot(linv_ref[...], mine_ref[...] + far_ref[...]) * (1.0 / replicas)


def q_half(mine, far, linv, replicas):
    return call(functools.partial(q_kernel, replicas), "q_half", (), (mine, far, linv), [(mine.shape, F32)])[0]


def error_block(part, k, block, q_ref, left_ref, moment_ref, right):
    rank, half = q_ref.shape
    here = pl.ds(k * block, block)
    cols = pl.ds(pl.multiple_of(part * half + k * block, block), block)
    hi, mid, lo = split3(-q_ref[:, here])
    for i, piece in enumerate((hi, mid, hi, mid, lo, hi)):
        right[i * rank : (i + 1) * rank, here] = piece
    return (moment_ref[:, cols] + dot_nn(left_ref[...], right[:, here])).astype(BF16)


def error_first_kernel(block, core_ref, q_ref, left_ref, moment_ref, out_ref, right):
    for k in range(q_ref.shape[1] // block):
        here = pl.ds(k * block, block)
        out_ref[:, here] = error_block(core_ref[0], k, block, q_ref, left_ref, moment_ref, right)


def error_first(core, q, left, moment):
    half = q.shape[1]
    return call(
        functools.partial(error_first_kernel, 512),
        "new_error_first",
        (core,),
        (q, left, moment),
        [((moment.shape[0], half), BF16)],
        [pltpu.VMEM((left.shape[1], half), BF16)],
        flops=10**10,
    )[0]


def last_kernel(block, parts, core_ref, mine_ref, other_ref, left_ref, moment_ref, first_ref, *rest):
    count = len(rest) - (10 if parts else 5)
    chunks = rest[2 : 2 + count] if parts else ()
    near_ref, pick_ref = rest[:2] if parts else (None, None)
    outs = rest[2 + count :] if parts else rest
    q_hbm, out_hbm = outs[:2]
    right, held, sems = outs[-3:]
    half = mine_ref.shape[1]
    part = 1 - core_ref[0]
    at_mine = pl.ds(pl.multiple_of(core_ref[0] * half, half), half)
    at_other = pl.ds(pl.multiple_of(part * half, half), half)
    copies = [
        pltpu.make_async_copy(first_ref, out_hbm.at[:, at_mine], sems.at[0]),
        pltpu.make_async_copy(mine_ref, q_hbm.at[:, at_mine], sems.at[1]),
        pltpu.make_async_copy(other_ref, q_hbm.at[:, at_other], sems.at[2]),
    ]
    for copy in copies:
        copy.start()
    steps = half // block
    for k in range(steps):
        here = pl.ds(k * block, block)
        cols = pl.ds(pl.multiple_of(part * half + k * block, block), block)
        held[:, here] = error_block(part, k, block, other_ref, left_ref, moment_ref, right)
        copies.append(pltpu.make_async_copy(held.at[:, here], out_hbm.at[:, cols], sems.at[3 + k]))
        copies[-1].start()
    if parts:
        grad_hbm, cat, grad_ref = outs[2:5]
        cap = chunks[0].shape[0]
        for k in range(count):
            cat[k * cap : (k + 1) * cap, :] = chunks[k][...]
        rows = grad_ref.shape[0] // parts
        for k in range(parts):
            at = pl.ds(k * rows, rows)
            grad_ref[at, :] = near_ref[at, :] + dot_nn(pick_ref[at, :], cat[...]).astype(BF16)
            copies.append(pltpu.make_async_copy(grad_ref.at[at, :], grad_hbm.at[at, :], sems.at[3 + steps + k]))
            copies[-1].start()
    for copy in copies:
        copy.wait()


def last_part(core, mine, other, left, moment, first, near=None, pick=None, chunks=()):
    ff, width = moment.shape
    rank, half = mine.shape
    block = 512
    parts = 2 if chunks else 0
    operands = [mine, other, left, moment, first]
    outs = [((rank, width), F32), ((ff, width), BF16)]
    scratch = []
    if chunks:
        operands += [near, pick, *chunks]
        outs.append((near.shape, BF16))
        scratch = [pltpu.VMEM((pick.shape[1], ff), BF16), pltpu.VMEM(near.shape, BF16)]
    scratch += [
        pltpu.VMEM((left.shape[1], half), BF16),
        pltpu.VMEM((ff, half), BF16),
        pltpu.SemaphoreType.DMA((3 + half // block + parts,)),
    ]
    return call(
        functools.partial(last_kernel, block, parts),
        "new_error_last",
        (core,),
        operands,
        outs,
        scratch,
        out_specs=[in_hbm()] * len(outs),
        flops=10**10,
    )


def pick_kernel(n, cap, masks, me_ref, counts_ref, order_ref, out_ref, held):
    order = order_ref[...]
    j = lax.broadcasted_iota(jnp.int32, (cap, order.shape[1]), 0)
    for k, mask in enumerate(masks):
        expert = me_ref[0] ^ mask
        start = jnp.int32(0)
        for e in range(n):
            start = start + jnp.where(e < expert, counts_ref[e], 0)
        hit = (order == j + start) & (j < counts_ref[expert])
        held[k * cap : (k + 1) * cap, :] = jnp.where(hit, 1.0, 0.0)
    out_ref[...] = held[...].T.astype(BF16)


def pick_of(me, counts, order, n, cap, masks):
    tokens = order.shape[1]
    slots = len(masks) * cap
    return call(
        functools.partial(pick_kernel, n, cap, masks),
        "pick_rows",
        (me, counts),
        (order,),
        [((tokens, slots), BF16)],
        [pltpu.VMEM((slots, tokens), F32)],
        flops=10**6,
        nbytes=10**4,
    )[0]


def unpack_first_kernel(count, before_ref, pick_ref, *rest):
    chunks, (out_ref, token_ref, cat) = rest[:count], rest[count:]
    cap = chunks[0].shape[0]
    for k in range(count):
        cat[k * cap : (k + 1) * cap, :] = chunks[k][...]
    out_ref[...] = dot_nn(pick_ref[...], cat[...]).astype(BF16)
    set_token(token_ref)


def unpack_first(before, pick, chunks):
    cap, ff = chunks[0].shape
    return call(
        functools.partial(unpack_first_kernel, len(chunks)),
        "unpack_first",
        (),
        (before, pick, *chunks),
        [((pick.shape[0], ff), BF16), TOKEN],
        [pltpu.VMEM((len(chunks) * cap, ff), BF16)],
        flops=10**10,
    )


def pack_plain(route_count, local_rows, experts, capacity):
    total_rows, width = local_rows.shape
    route_starts = jnp.cumsum(route_count) - route_count
    slot_ids = jnp.arange(capacity, dtype=jnp.int32)
    pick_index = jnp.minimum(route_starts[:, None] + slot_ids[None, :], total_rows - 1)
    slot_valid = slot_ids[None, :] < route_count[:, None]
    outgoing = local_rows[pick_index.reshape(-1)].reshape(experts, capacity, width)
    return jnp.where(slot_valid[:, :, None], outgoing, jnp.zeros((), BF16))


def unpack_plain(route_count, order_local, returned, experts, capacity):
    route_ends = jnp.cumsum(route_count)
    route_starts = route_ends - route_count
    expert_of = jnp.sum((route_ends[None, :] <= order_local[:, None]).astype(jnp.int32), axis=1)
    row_base = jnp.arange(experts, dtype=jnp.int32) * capacity - route_starts
    return returned[row_base[expert_of] + order_local]


def gap_kernel(*refs):
    set_token(refs[-1])


def gap(*before):
    return call(gap_kernel, "gap", (), before, [TOKEN], limit=4, flops=10**10)[0]


def add_kernel(a_ref, b_ref, *rest):
    rest[-1][...] = a_ref[...] + b_ref[...]


def add(a, b, *before):
    return call(add_kernel, "add", (), (a, b, *before), [(a.shape, F32)], limit=4, flops=10**6)[0]


def pass_kernel(x_ref, before_ref, out_ref):
    out_ref[...] = x_ref[...]


def pass_on(x, before):
    return call(pass_kernel, "pass_on", (), (x, before), [(x.shape, x.dtype)], limit=4, flops=10**6)[0]


def shards(n_expert, n_dp, grad_rows, counts, order, hidden, down_weight, error_in, q_init):
    rows = grad_rows[0]
    count = counts[0, 0]
    saved = hidden[0, 0]
    weight = down_weight[0]
    error = error_in[0, 0]
    q = q_init[0].T
    ff = saved.shape[1]
    capacity = saved.shape[0] // n_expert
    me = lax.axis_index("expert").astype(jnp.int32)[None]
    core = (lax.axis_index("dp").astype(jnp.int32) & 1)[None]
    core_pairs = [(d, d ^ 1) for d in range(n_dp)]
    chip_pairs = [(d, d ^ 2) for d in range(n_dp)]
    by_pairs = n_expert == 8 and capacity % ROW_TILE == 0 and rows.shape[0] % ROW_TILE == 0

    if by_pairs:
        far = tuple(reversed(range(n_expert // 2, n_expert)))
        near = tuple(reversed(range(0, n_expert // 2)))
        first, last = far[:1] + near, far[1:]

        def swap(x, mask):
            return lax.ppermute(x, "expert", [(e, e ^ mask) for e in range(n_expert)])

        others = far[1:] + near
        packed = {far[0]: pack_first(me, core, counts[0], rows, n_expert, capacity, far[0])}
        packed.update(zip(others, pack(me, counts[0], rows, n_expert, capacity, others)))
        arrived = {m: swap(packed[m], m) if m else packed[m] for m in far + near}
        pick_near = pick_of(me, count, order, n_expert, capacity, near)
        pick_far = pick_of(me, count, order, n_expert, capacity, far)
        p_first, both_first, moment, *back = early_part(
            me, q, saved, error, weight, [arrived[m] for m in first], first
        )
        back_near = [swap(x, m) if m else x for x, m in zip(back[1:], near)]
        p_mine, both_last = late_part(me, weight, q, saved, p_first, [arrived[m] for m in last], last)
        back_soon = pass_on(back[0], p_mine)
        before = [gap(p_mine, pick_near, pick_far, *back_near)]
        groups = [both_first, both_last]
    else:
        outgoing = pack_plain(count, rows, n_expert, capacity)
        arrived = lax.all_to_all(outgoing, "expert", split_axis=0, concat_axis=0, tiled=True)
        arrived = arrived.reshape(n_expert * capacity, rows.shape[1])
        p_mine, both_first, moment, back = early_part(me, q, saved, error, weight, [arrived], (None,))
        before, groups = [], [both_first]
        back = back.reshape(n_expert, capacity, ff)
        returned = lax.all_to_all(back, "expert", split_axis=0, concat_axis=0, tiled=True)
        returned = returned.reshape(n_expert * capacity, ff)
    p_chip = add(p_mine, lax.ppermute(p_mine, "dp", core_pairs), *before)
    p_far = lax.ppermute(p_chip, "dp", chip_pairs)
    before = p_chip
    if by_pairs:
        back_next = slot_grads(both_last, weight, (p_chip,), 0, capacity, len(last), 10**6)
        moment = moment_add(back_next[0], moment, both_last)
        before = back_next[0]
    p_total, s_sent, p3, *ys = s_send(core, before, p_chip, p_far, error, groups)
    s_swapped = lax.ppermute(s_sent, "dp", core_pairs)
    s_kept, token = s_keep(core, p3, ys, error, groups)
    if by_pairs:
        grad_near, token = unpack_first(token, pick_near, back_near)
    s_half = add(s_kept, s_swapped, token)
    if by_pairs:
        back_last = pass_on(back_next[-1], s_half)
        back_far = [swap(x, m) for x, m in zip([back_soon, *back_next[:-1], back_last], far)]
    basis, linv, left = basis_of(p_total, back_last if by_pairs else p_total)
    q_mine = q_half(s_half, lax.ppermute(s_half, "dp", chip_pairs), linv, n_dp)
    q_other = lax.ppermute(q_mine, "dp", core_pairs)
    first_half = error_first(core, q_mine, left, moment)
    if by_pairs:
        q_factor, error_out, input_grad = last_part(
            core, q_mine, q_other, left, moment, first_half, grad_near, pick_far, back_far
        )
    else:
        q_factor, error_out = last_part(core, q_mine, q_other, left, moment, first_half)
        input_grad = unpack_plain(count, order[0], returned, n_expert, capacity)
    return (input_grad[None], basis.T[None], q_factor.T[None], error_out[None, None])


def solution(mesh):
    placed = (
        P("dp", "expert", None),
        P("dp", "expert", None),
        P("dp", "expert"),
        P("dp", "expert", None, None),
        P("expert", None, None),
        P("dp", "expert", None, None),
        P("expert", None, None),
    )
    return jax.shard_map(
        functools.partial(shards, mesh.shape["expert"], mesh.shape["dp"]),
        mesh=mesh,
        in_specs=placed,
        out_specs=(
            P("dp", "expert", None),
            P("expert", None, None),
            P("expert", None, None),
            P("dp", "expert", None, None),
        ),
        check_vma=False,
    )
```
